256 devices in a mesh: row: 8 (over z), col: 16 (over x, y), layer: 2 (over core).
Axes of the slice: x: 4, y: 4, z: 8, core: 2. Of those that a mesh axis runs over, the one named last changes fastest.
Arguments:
- coeffs: bfloat16 [16384, 4096], P('row', 'col'), may hold values from -6 to 6
- block_sizes: int32 [128], P('row'), may hold values from 64 to 128, as said below
- neighbours: int32 [128, 16], P('row'), may hold values from 0 to 127, as said below
- ham_blocks: bfloat16 [128, 16, 128, 128], P('row', 'layer'), may hold values from -0.125 to 0.125
- ovl_blocks: bfloat16 [128, 16, 128, 128], P('row', 'layer'), may hold values from -0.125 to 0.125
Outputs:
- residual: float32 [16384, 4096], P(('row', 'layer'), 'col')
The draws below stay inside these ranges and needn't reach their ends.
Inputs may be any that keep to these rules, and one draw needn't show every extreme that they name: `block_sizes`: some block has exactly 128 live basis functions. `neighbours`: every entry names a block at most 16 blocks from its row's block; slot 0 names the row's own block.
All inputs are finite; a program needn't handle non-finite values.
Results may differ from the reference program's by a relative error of at most 0.0031.
Values may be sent and summed in bfloat16 or wider, within the bound.
A program may use at most 128 MiB of HBM per device.

```python
import jax
import jax.numpy as jnp
from jax import lax

B = 128
NOCC = 4096
K = 16
NBR = 16
NB = 128
ROWS = 16384


def draw_block_sizes(key, part):
    sizes = jax.random.randint(key, (NB,), B // 2, B + 1).astype(jnp.int32)
    where = jax.random.randint(jax.random.fold_in(key, 7), (), 0, NB)
    return sizes.at[where].set(B).astype(jnp.int32)


def draw_neighbours(key, part):
    offsets = jax.random.randint(key, (NB, K), -NBR, NBR + 1)
    own = jnp.arange(NB, dtype=jnp.int32)
    picked = jnp.clip(own[:, None] + offsets, 0, NB - 1)
    return picked.at[:, 0].set(own).astype(jnp.int32)


def block_scale(stream_key, dims, shards, smallest, largest):
    loudness = 1.0
    for position, blocks in shards:
        steps = jax.random.uniform(jax.random.fold_in(jax.random.fold_in(stream_key, 6), position), (blocks,), jnp.float32, smallest / len(shards), largest / len(shards))
        loudness = loudness * jnp.repeat(jnp.exp(steps), dims[position] // blocks).reshape((-1,) + (1,) * (len(dims) - 1 - position))
    return loudness


def centred(stream_key, dims, width, reach, shards=(), kind=jnp.bfloat16):
    gain = block_scale(stream_key, dims, shards, -0.22, 0.18) if shards else 1.0
    entries = jax.random.normal(stream_key, dims, jnp.float32) * width * gain
    return jnp.minimum(jnp.maximum(entries, -reach), reach).astype(kind)


def setup_inputs(seed: int = 0) -> dict:
    arg_keys = jax.random.split(jax.random.key(seed), 6)
    coeffs = centred(arg_keys[0], (ROWS, NOCC), 1.0, 6.0, ((0, 8), (1, 16)))
    block_sizes = draw_block_sizes(jax.random.fold_in(arg_keys[5], 71), 0)
    neighbours = draw_neighbours(jax.random.fold_in(arg_keys[5], 71), 0)
    ham_blocks = centred(arg_keys[3], (NB, K, B, B), (K * B) ** -0.5, 0.125, ((0, 8), (1, 2)))
    ovl_blocks = centred(arg_keys[4], (NB, K, B, B), (K * B) ** -0.5, 0.125, ((0, 8), (1, 2)))
    return dict(coeffs=coeffs, block_sizes=block_sizes, neighbours=neighbours, ham_blocks=ham_blocks, ovl_blocks=ovl_blocks)


def reference(coeffs, block_sizes, neighbours, ham_blocks, ovl_blocks):
    count_blocks = block_sizes.shape[0]
    block_rows = ham_blocks.shape[2]
    live = (jnp.arange(block_rows, dtype=jnp.int32)[None, :] < block_sizes[:, None])
    cblocks = coeffs.reshape(count_blocks, block_rows, -1) * live[:, :, None].astype(coeffs.dtype)

    def one_row(items):
        hrow, srow, nrow, lrow = items
        picked = cblocks[nrow].astype(jnp.float32)
        wpart = jnp.einsum('kpq,kqn->pn', hrow.astype(jnp.float32), picked) * lrow[:, None]
        vpart = jnp.einsum('kpq,kqn->pn', srow.astype(jnp.float32), picked) * lrow[:, None]
        return wpart.astype(jnp.bfloat16), vpart.astype(jnp.bfloat16)

    hc, sc = lax.map(one_row, (ham_blocks, ovl_blocks, neighbours, live.astype(jnp.float32)))
    total_rows = count_blocks * block_rows
    hc = hc.reshape(total_rows, -1)
    sc = sc.reshape(total_rows, -1)
    masked = cblocks.reshape(total_rows, -1)
    gram = (jnp.dot(masked.T, hc, preferred_element_type=jnp.float32) / total_rows).astype(jnp.bfloat16)
    return hc.astype(jnp.float32) - jnp.dot(sc, gram, preferred_element_type=jnp.float32)
```

```python
import jax
import jax.numpy as jnp
from jax import lax
from jax.experimental import pallas as pl
from jax.experimental.pallas import tpu as pltpu
from jax.sharding import PartitionSpec as P

MESH = pl.DeviceIdType.MESH
BF = jnp.bfloat16
F32 = jnp.float32
GROUPS = ((0, 1), (2, 3))


def kernel(
    sizes, neigh, coeffs, ham, ovl, out,
    raw, cbuf, hbuf, sbuf, ctg, hcg, scg, gown, gsend, grecv, gram,
    rs_s, rs_r, rs_s4, rs_r4, opp_s, opp_r, nb_s, nb_r, racc,
    loc, zs, zr, hs, hr, ys, yr, xs, xr, ss, sr, ps, pr,
    rss, rsr, ags, agr, agps, agpr, fs, fr,
):
    z = lax.axis_index("row")
    col = lax.axis_index("col")
    l = lax.axis_index("layer")
    x, y = col // 4, col % 4
    here = (z, col, l)
    up = (lax.rem(z + 1, 8), col, l)
    down = (lax.rem(z + 7, 8), col, l)
    xr_dev = (z, lax.rem(x + 1, 4) * 4 + y, l)
    xl_dev = (z, lax.rem(x + 3, 4) * 4 + y, l)
    yr_dev = (z, x * 4 + lax.rem(y + 1, 4), l)
    yl_dev = (z, x * 4 + lax.rem(y + 3, 4), l)
    twin = (z, col, 1 - l)
    del here

    def remote(src, dst, s, r, device):
        return pltpu.make_async_remote_copy(
            src_ref=src, dst_ref=dst, send_sem=s, recv_sem=r, device_id=device, device_id_type=MESH
        )

    sent = []

    def send(src, dst, s, r, device):
        copy = remote(src, dst, s, r, device)
        copy.start()
        sent.append(copy)
        return copy

    load = pltpu.make_async_copy(coeffs, raw, loc.at[0])
    load.start()
    barrier = pltpu.get_barrier_semaphore()
    for device in (up, down, xr_dev, xl_dev, yr_dev, yl_dev, twin):
        pl.semaphore_signal(barrier, inc=1, device_id=device, device_id_type=MESH)
    own_h = pltpu.make_async_copy(
        ham.at[pl.ds(l * 8, 8)], hbuf.at[:, pl.ds(l * 8, 8)], loc.at[1]
    )
    own_s = pltpu.make_async_copy(
        ovl.at[pl.ds(l * 8, 8)], sbuf.at[:, pl.ds(l * 8, 8)], loc.at[2]
    )
    load.wait()

    def mask_block(b):
        block = raw[pl.ds(b * 128, 128), :].astype(F32)
        rows = lax.broadcasted_iota(jnp.int32, (128, 256), 0)
        cbuf[16 + b] = jnp.where(rows < sizes[b], block, 0.0).astype(BF)

    @pl.loop(0, 8)
    def _(i):
        mask_block(l * 8 + i)

    pl.semaphore_wait(barrier, 7)

    mine = cbuf.at[pl.ds(16 + l * 8, 8)]
    to_up = send(mine, cbuf.at[pl.ds(l * 8, 8)], zs.at[0], zr.at[0], up)
    to_down = send(mine, cbuf.at[pl.ds(32 + l * 8, 8)], zs.at[1], zr.at[1], down)
    give_h = send(
        ham.at[pl.ds((1 - l) * 8, 8)], hbuf.at[:, pl.ds(l * 8, 8)], hs.at[0], hr.at[0], twin
    )
    own_h.start()

    @pl.loop(0, 8)
    def _(i):
        ctg[y, :, pl.ds(pl.multiple_of(i * 128, 128), 128)] = cbuf[16 + l * 8 + i].T

    def ring4(buf, me, half, s, r, right, left):
        a, b = pl.ds(0, half), pl.ds(half, half)
        fa = lax.rem(me + 3, 4)
        fb = lax.rem(me + 1, 4)
        ra = send(buf.at[me, a], buf.at[me, a], s.at[0], r.at[0], right)
        lb = send(buf.at[me, b], buf.at[me, b], s.at[1], r.at[1], left)
        yield
        rb = send(buf.at[me, b], buf.at[me, b], s.at[2], r.at[2], right)
        la = send(buf.at[me, a], buf.at[me, a], s.at[3], r.at[3], left)
        yield
        ra.wait_recv()
        fra = send(buf.at[fa, a], buf.at[fa, a], s.at[4], r.at[4], right)
        lb.wait_recv()
        flb = send(buf.at[fb, b], buf.at[fb, b], s.at[5], r.at[5], left)
        yield
        rb.wait_recv()
        la.wait_recv()
        yield
        fra.wait_recv()
        flb.wait_recv()
        yield

    yring = ring4(ctg, y, 128, ys, yr, yr_dev, yl_dev)
    next(yring)
    next(yring)
    give_s = send(
        ovl.at[pl.ds((1 - l) * 8, 8)], sbuf.at[:, pl.ds(l * 8, 8)], hs.at[1], hr.at[1], twin
    )
    own_s.start()

    @pl.loop(0, 8)
    def _(i):
        mask_block((1 - l) * 8 + i)

    next(yring)
    to_up.wait_recv()
    to_down.wait_recv()
    hand = jnp.where(l == 0, 32, 8)
    take = send(cbuf.at[pl.ds(hand, 8)], cbuf.at[pl.ds(hand, 8)], zs.at[2], zr.at[2], twin)
    own_h.wait()
    give_h.wait_recv()
    take.wait_recv()

    first = z * 16 - 16

    def picked(b, k):
        return cbuf[jnp.clip(neigh[b, k] - first, 0, 47)]

    def spmm(blocks, store, begin, end):
        @pl.loop(begin, end)
        def _(i):
            b = l * 8 + i
            total = jnp.zeros((128, 256), F32)
            for k in range(0, 16, 2):
                lhs = jnp.concatenate([blocks[i, k], blocks[i, k + 1]], axis=1)
                rhs = jnp.concatenate([picked(b, k), picked(b, k + 1)], axis=0)
                total += jnp.dot(lhs, rhs, preferred_element_type=F32)
            rows = lax.broadcasted_iota(jnp.int32, (128, 256), 0)
            store[pl.ds(pl.multiple_of(i * 128, 128), 128), :] = jnp.where(
                rows < sizes[b], total, 0.0
            ).astype(BF)

    spmm(hbuf, hcg.at[x], 0, 8)
    xring = ring4(hcg, x, 512, xs, xr, xr_dev, xl_dev)
    next(xring)
    next(xring)
    next(yring)
    next(yring)
    own_s.wait()
    give_s.wait_recv()
    spmm(sbuf, scg.at[y], 0, 8)
    sring = ring4(scg, y, 512, ss, sr, yr_dev, yl_dev)
    next(sring)
    next(sring)

    slots = (x, lax.rem(x + 2, 4), lax.rem(x + 1, 4), lax.rem(x + 3, 4))
    swaps = {}

    def gram_part(p):
        rhs = hcg.at[slots[p]]

        @pl.loop(0, 2)
        def _(i):
            gsend[p, pl.ds(pl.multiple_of(i * 256, 256), 256), :] = jnp.dot(
                ctg[(1 - l) * 2 + i], rhs[...], preferred_element_type=F32
            )

        swaps[p] = send(gsend.at[p], grecv.at[p], ps.at[p], pr.at[p], twin)

        @pl.loop(0, 2)
        def _(i):
            gown[p, pl.ds(pl.multiple_of(i * 256, 256), 256), :] = jnp.dot(
                ctg[l * 2 + i], rhs[...], preferred_element_type=F32
            )

    def gram_add(p):
        swaps[p].wait_recv()
        gown[p] = gown[p] + grecv[p]

    def part(g, d):
        c = lax.rem(z + 8 + d, 8)
        return gown[g[0] : g[-1] + 1, pl.ds(pl.multiple_of(c * 64, 64), 64), :]

    def z_reduce(gi):
        g = GROUPS[gi]
        where = pl.ds(g[0], len(g))
        for p in g:
            gram_add(p)
        rs_s4[0, where] = part(g, 4)[:, :, :128].astype(BF)
        rs_s4[1, where] = part(g, 4)[:, :, 128:].astype(BF)
        right = send(rs_s4.at[0, where], rs_r4.at[0, where], rss.at[gi, 0], rsr.at[gi, 0], up)
        left = send(rs_s4.at[1, where], rs_r4.at[1, where], rss.at[gi, 1], rsr.at[gi, 1], down)
        for k in range(3):
            yield
            d = 3 - k
            right.wait_recv()
            term = part(g, d)
            if k == 0:
                rs_s[k, 0, where, :, :128] = (
                    term[:, :, :128] + rs_r4[0, where].astype(F32)
                ).astype(BF)
                rs_s[k, 0, where, :, 128:] = term[:, :, 128:].astype(BF)
            else:
                rs_s[k, 0, where] = (term + rs_r[k - 1, 0, where].astype(F32)).astype(BF)
            right = send(
                rs_s.at[k, 0, where], rs_r.at[k, 0, where],
                rss.at[gi, 2 * k + 2], rsr.at[gi, 2 * k + 2], up,
            )
            left.wait_recv()
            term = part(g, -d)
            if k == 0:
                rs_s[k, 1, where, :, 128:] = (
                    term[:, :, 128:] + rs_r4[1, where].astype(F32)
                ).astype(BF)
                rs_s[k, 1, where, :, :128] = term[:, :, :128].astype(BF)
            else:
                rs_s[k, 1, where] = (term + rs_r[k - 1, 1, where].astype(F32)).astype(BF)
            left = send(
                rs_s.at[k, 1, where], rs_r.at[k, 1, where],
                rss.at[gi, 2 * k + 3], rsr.at[gi, 2 * k + 3], down,
            )
        yield
        right.wait_recv()
        left.wait_recv()
        whole = part(g, 0) + rs_r[2, 0, where].astype(F32) + rs_r[2, 1, where].astype(F32)

        def rows(d):
            c = lax.rem(z + 8 + d, 8)
            return pl.ds(pl.multiple_of(l * 512 + c * 64, 64), 64)

        gram[where, rows(0), :] = (whole * (1.0 / 16384.0)).astype(BF)
        twins = []

        def to_twin(d, n):
            ref = gram.at[where, rows(d), :]
            twins.append(send(ref, ref, agps.at[gi, n], agpr.at[gi, n], twin))

        def hop(d, n, device, cols=slice(None)):
            ref = gram.at[where, rows(d), cols]
            return send(ref, ref, ags.at[gi, n], agr.at[gi, n], device)

        right = hop(0, 0, up)
        left = hop(0, 1, down)
        to_twin(0, 0)
        for k in range(1, 4):
            yield
            right.wait_recv()
            right = hop(-k, 2 * k, up, slice(None) if k < 3 else pl.ds(0, 128))
            to_twin(-k, 2 * k - 1)
            left.wait_recv()
            left = hop(k, 2 * k + 1, down, slice(None) if k < 3 else pl.ds(128, 128))
            to_twin(k, 2 * k)
        yield
        right.wait_recv()
        left.wait_recv()
        to_twin(4, 7)
        yield
        for copy in twins:
            copy.wait_recv()
        yield

    def drain(gen):
        for _ in gen:
            pass

    gram_part(0)
    next(xring)
    next(sring)
    next(xring)
    next(xring)
    gram_part(1)
    zr0 = z_reduce(0)
    next(zr0)
    gram_part(2)
    gram_part(3)
    next(zr0)
    zr1 = z_reduce(1)
    next(zr1)
    next(zr0)
    next(zr1)
    next(sring)
    next(sring)
    for _ in range(8):
        next(zr0, None)
        next(zr1, None)
    drain(zr0)

    def project(p, i):
        total = jnp.zeros((512, 256), F32)
        for k in range(4):
            total += jnp.dot(
                scg[k, pl.ds(i * 512, 512), :], gram[p, k * 256 : (k + 1) * 256, :],
                preferred_element_type=F32,
            )
        return total

    opp_s[0] = project(1, 0).astype(BF)
    far_r = send(opp_s.at[0], opp_r.at[0], fs.at[0], fr.at[0], xr_dev)
    opp_s[1] = project(1, 1).astype(BF)
    far_l = send(opp_s.at[1], opp_r.at[1], fs.at[1], fr.at[1], xl_dev)
    drain(zr1)
    nb_s[0, 1] = project(2, 1).astype(BF)
    near = [send(nb_s.at[0, 1], nb_r.at[0, 1], fs.at[2], fr.at[2], xr_dev)]
    nb_s[1, 0] = project(3, 0).astype(BF)
    near.append(send(nb_s.at[1, 0], nb_r.at[1, 0], fs.at[3], fr.at[3], xl_dev))
    racc[0] = project(2, 0)
    racc[1] = project(3, 1)
    far_r.wait_recv()
    nb_s[0, 0] = (racc[0] + opp_r[0].astype(F32)).astype(BF)
    near.append(send(nb_s.at[0, 0], nb_r.at[0, 0], fs.at[4], fr.at[4], xr_dev))
    far_l.wait_recv()
    nb_s[1, 1] = (racc[1] + opp_r[1].astype(F32)).astype(BF)
    near.append(send(nb_s.at[1, 1], nb_r.at[1, 1], fs.at[5], fr.at[5], xl_dev))
    for i in range(2):
        racc[i] = hcg[x, pl.ds(i * 512, 512), :].astype(F32) - project(0, i)
    for copy in near:
        copy.wait_recv()
    for i in range(2):
        out[pl.ds(i * 512, 512), :] = racc[i] - nb_r[0, i].astype(F32) - nb_r[1, i].astype(F32)
    for copy in sent:
        copy.wait_send()


def body(coeffs, block_sizes, neighbours, ham_blocks, ovl_blocks):
    vmem = pltpu.VMEM
    dma = pltpu.SemaphoreType.DMA
    n = len(GROUPS)
    smem = pl.BlockSpec(memory_space=pltpu.SMEM)
    hbm = pl.BlockSpec(memory_space=pl.ANY)
    return pl.pallas_call(
        kernel,
        out_shape=jax.ShapeDtypeStruct((1024, 256), F32),
        in_specs=[smem, smem, hbm, hbm, hbm],
        out_specs=pl.BlockSpec(memory_space=pltpu.VMEM),
        scratch_shapes=[
            vmem((2048, 256), BF),
            vmem((48, 128, 256), BF),
            vmem((8, 16, 128, 128), BF),
            vmem((8, 16, 128, 128), BF),
            vmem((4, 256, 1024), BF),
            vmem((4, 1024, 256), BF),
            vmem((4, 1024, 256), BF),
            vmem((4, 512, 256), F32),
            vmem((4, 512, 256), F32),
            vmem((4, 512, 256), F32),
            vmem((4, 1024, 256), BF),
            vmem((3, 2, 4, 64, 256), BF),
            vmem((3, 2, 4, 64, 256), BF),
            vmem((2, 4, 64, 128), BF),
            vmem((2, 4, 64, 128), BF),
            vmem((2, 512, 256), BF),
            vmem((2, 512, 256), BF),
            vmem((2, 2, 512, 256), BF),
            vmem((2, 2, 512, 256), BF),
            vmem((2, 512, 256), F32),
            dma((3,)),
            dma((3,)), dma((3,)),
            dma((2,)), dma((2,)),
            dma((6,)), dma((6,)),
            dma((6,)), dma((6,)),
            dma((6,)), dma((6,)),
            dma((4,)), dma((4,)),
            dma((n, 8)), dma((n, 8)),
            dma((n, 8)), dma((n, 8)),
            dma((n, 8)), dma((n, 8)),
            dma((6,)), dma((6,)),
        ],
        compiler_params=pltpu.CompilerParams(
            collective_id=0, has_side_effects=True, vmem_limit_bytes=56 * 2**20
        ),
        cost_estimate=pl.CostEstimate(
            flops=6 * 2**30, bytes_accessed=12 * 2**20, transcendentals=0
        ),
        name="block_sparse_residual",
    )(block_sizes, neighbours, coeffs, ham_blocks, ovl_blocks)


def solution(mesh):
    return jax.shard_map(
        body,
        mesh=mesh,
        in_specs=(
            P("row", "col"),
            P("row"),
            P("row", None),
            P("row", "layer", None, None),
            P("row", "layer", None, None),
        ),
        out_specs=P(("row", "layer"), "col"),
        check_vma=False,
    )
```

```python
import jax
import jax.numpy as jnp
from jax import lax
from jax.experimental import pallas as pl
from jax.experimental.pallas import tpu as pltpu
from jax.sharding import PartitionSpec as P

MESH = pl.DeviceIdType.MESH
BF = jnp.bfloat16
F32 = jnp.float32
GROUPS = ((0,), (1,), (2,), (3,))


def kernel(
    sizes, neigh, coeffs, ham, ovl, out,
    raw, cbuf, hbuf, sbuf, ctg, hcg, scg, gown, gsend, grecv, gram,
    rs_s, rs_r, rs_s4, rs_r4, opp_s, opp_r, nb_s, nb_r, racc, own,
    loc, zs, zr, hs, hr, ys, yr, xs, xr, ss, sr, ps, pr,
    rss, rsr, ags, agr, agps, agpr, fs, fr,
):
    z = lax.axis_index("row")
    col = lax.axis_index("col")
    l = lax.axis_index("layer")
    x, y = col // 4, col % 4
    here = (z, col, l)
    up = (lax.rem(z + 1, 8), col, l)
    down = (lax.rem(z + 7, 8), col, l)
    xr_dev = (z, lax.rem(x + 1, 4) * 4 + y, l)
    xl_dev = (z, lax.rem(x + 3, 4) * 4 + y, l)
    yr_dev = (z, x * 4 + lax.rem(y + 1, 4), l)
    yl_dev = (z, x * 4 + lax.rem(y + 3, 4), l)
    twin = (z, col, 1 - l)
    del here

    def remote(src, dst, s, r, device):
        return pltpu.make_async_remote_copy(
            src_ref=src, dst_ref=dst, send_sem=s, recv_sem=r, device_id=device, device_id_type=MESH
        )

    sent = []

    def gone(copy):
        copy.wait_send()
        sent[:] = [other for other in sent if other is not copy]

    def send(src, dst, s, r, device):
        copy = remote(src, dst, s, r, device)
        copy.start()
        sent.append(copy)
        return copy

    load = pltpu.make_async_copy(coeffs, raw, loc.at[0])
    load.start()
    barrier = pltpu.get_barrier_semaphore()
    for device in (up, down, xr_dev, xl_dev, yr_dev, yl_dev, twin):
        pl.semaphore_signal(barrier, inc=1, device_id=device, device_id_type=MESH)
    own_h = pltpu.make_async_copy(
        ham.at[pl.ds(l * 8, 8)], hbuf.at[:, pl.ds(l * 8, 8)], loc.at[1]
    )
    own_s = pltpu.make_async_copy(
        ovl.at[pl.ds(l * 8, 8)], sbuf.at[:, pl.ds(l * 8, 8)], loc.at[2]
    )
    load.wait()

    def mask_block(b):
        block = raw[pl.ds(b * 128, 128), :].astype(F32)
        rows = lax.broadcasted_iota(jnp.int32, (128, 256), 0)
        cbuf[16 + b] = jnp.where(rows < sizes[b], block, 0.0).astype(BF)

    @pl.loop(0, 8)
    def _(i):
        mask_block(l * 8 + i)

    pl.semaphore_wait(barrier, 7)

    mine = cbuf.at[pl.ds(16 + l * 8, 8)]
    to_up = send(mine, cbuf.at[pl.ds(l * 8, 8)], zs.at[0], zr.at[0], up)
    to_down = send(mine, cbuf.at[pl.ds(32 + l * 8, 8)], zs.at[1], zr.at[1], down)
    give_h = send(
        ham.at[pl.ds((1 - l) * 8, 8)], hbuf.at[:, pl.ds(l * 8, 8)], hs.at[0], hr.at[0], twin
    )
    own_h.start()

    @pl.loop(0, 8)
    def _(i):
        ctg[y, :, pl.ds(pl.multiple_of(i * 128, 128), 128)] = cbuf[16 + l * 8 + i].T

    def ring4(buf, me, half, s, r, right, left):
        a, b = pl.ds(0, half), pl.ds(half, half)
        fa = lax.rem(me + 3, 4)
        fb = lax.rem(me + 1, 4)
        ra = send(buf.at[me, a], buf.at[me, a], s.at[0], r.at[0], right)
        lb = send(buf.at[me, b], buf.at[me, b], s.at[1], r.at[1], left)
        yield
        rb = send(buf.at[me, b], buf.at[me, b], s.at[2], r.at[2], right)
        la = send(buf.at[me, a], buf.at[me, a], s.at[3], r.at[3], left)
        yield
        ra.wait_recv()
        fra = send(buf.at[fa, a], buf.at[fa, a], s.at[4], r.at[4], right)
        lb.wait_recv()
        flb = send(buf.at[fb, b], buf.at[fb, b], s.at[5], r.at[5], left)
        yield
        rb.wait_recv()
        la.wait_recv()
        yield
        fra.wait_recv()
        flb.wait_recv()
        yield

    def ring4x(buf, me, half, s, r, right, left):
        a, b = pl.ds(0, half), pl.ds(half, half)
        fa = lax.rem(me + 3, 4)
        fb = lax.rem(me + 1, 4)
        ra = send(buf.at[me, a], buf.at[me, a], s.at[0], r.at[0], right)
        yield
        lb = send(buf.at[me, b], buf.at[me, b], s.at[1], r.at[1], left)
        yield
        ra.wait_recv()
        fra = send(buf.at[fa, a], buf.at[fa, a], s.at[2], r.at[2], right)
        lb.wait_recv()
        flb = send(buf.at[fb, b], buf.at[fb, b], s.at[3], r.at[3], left)
        yield
        gone(fra)
        rb = send(buf.at[me, b], buf.at[me, b], s.at[4], r.at[4], right)
        gone(flb)
        la = send(buf.at[me, a], buf.at[me, a], s.at[5], r.at[5], left)
        yield
        fra.wait_recv()
        flb.wait_recv()
        yield
        rb.wait_recv()
        la.wait_recv()
        yield

    yring = ring4(ctg, y, 128, ys, yr, yr_dev, yl_dev)
    next(yring)
    next(yring)
    give_s = send(
        ovl.at[pl.ds((1 - l) * 8, 8)], sbuf.at[:, pl.ds(l * 8, 8)], hs.at[1], hr.at[1], twin
    )
    own_s.start()

    @pl.loop(0, 8)
    def _(i):
        mask_block((1 - l) * 8 + i)

    next(yring)
    to_up.wait_recv()
    to_down.wait_recv()
    hand = jnp.where(l == 0, 32, 8)
    take = send(cbuf.at[pl.ds(hand, 8)], cbuf.at[pl.ds(hand, 8)], zs.at[2], zr.at[2], twin)
    own_h.wait()
    give_h.wait_recv()
    take.wait_recv()

    first = z * 16 - 16

    def picked(b, k):
        return cbuf[jnp.clip(neigh[b, k] - first, 0, 47)]

    def spmm(blocks, store, begin, end):
        @pl.loop(begin, end)
        def _(i):
            b = l * 8 + i
            total = jnp.zeros((128, 256), F32)
            for k in range(0, 16, 2):
                lhs = jnp.concatenate([blocks[i, k], blocks[i, k + 1]], axis=1)
                rhs = jnp.concatenate([picked(b, k), picked(b, k + 1)], axis=0)
                total += jnp.dot(lhs, rhs, preferred_element_type=F32)
            rows = lax.broadcasted_iota(jnp.int32, (128, 256), 0)
            store[pl.ds(pl.multiple_of(i * 128, 128), 128), :] = jnp.where(
                rows < sizes[b], total, 0.0
            ).astype(BF)

    slots = (x, lax.rem(x + 2, 4), lax.rem(x + 1, 4), lax.rem(x + 3, 4))
    swaps = {}

    def gram_part(p):
        rhs = hcg.at[slots[p]]

        @pl.loop(0, 2)
        def _(i):
            gsend[p, pl.ds(pl.multiple_of(i * 256, 256), 256), :] = jnp.dot(
                ctg[(1 - l) * 2 + i], rhs[...], preferred_element_type=F32
            )

        swaps[p] = send(gsend.at[p], grecv.at[p], ps.at[p], pr.at[p], twin)

        @pl.loop(0, 2)
        def _(i):
            gown[p, pl.ds(pl.multiple_of(i * 256, 256), 256), :] = jnp.dot(
                ctg[l * 2 + i], rhs[...], preferred_element_type=F32
            )

    def gram_add(p):
        swaps[p].wait_recv()
        gown[p] = gown[p] + grecv[p]

    def part(g, d):
        c = lax.rem(z + 8 + d, 8)
        return gown[g[0] : g[-1] + 1, pl.ds(pl.multiple_of(c * 64, 64), 64), :]

    def z_reduce(gi):
        g = GROUPS[gi]
        where = pl.ds(g[0], len(g))
        for p in g:
            gram_add(p)
        rs_s4[0, where] = part(g, 4)[:, :, :128].astype(BF)
        rs_s4[1, where] = part(g, 4)[:, :, 128:].astype(BF)
        right = send(rs_s4.at[0, where], rs_r4.at[0, where], rss.at[gi, 0], rsr.at[gi, 0], up)
        left = send(rs_s4.at[1, where], rs_r4.at[1, where], rss.at[gi, 1], rsr.at[gi, 1], down)
        for k in range(3):
            yield
            d = 3 - k
            right.wait_recv()
            term = part(g, d)
            if k == 0:
                rs_s[k, 0, where, :, :128] = (
                    term[:, :, :128] + rs_r4[0, where].astype(F32)
                ).astype(BF)
                rs_s[k, 0, where, :, 128:] = term[:, :, 128:].astype(BF)
            else:
                rs_s[k, 0, where] = (term + rs_r[k - 1, 0, where].astype(F32)).astype(BF)
            right = send(
                rs_s.at[k, 0, where], rs_r.at[k, 0, where],
                rss.at[gi, 2 * k + 2], rsr.at[gi, 2 * k + 2], up,
            )
            left.wait_recv()
            term = part(g, -d)
            if k == 0:
                rs_s[k, 1, where, :, 128:] = (
                    term[:, :, 128:] + rs_r4[1, where].astype(F32)
                ).astype(BF)
                rs_s[k, 1, where, :, :128] = term[:, :, :128].astype(BF)
            else:
                rs_s[k, 1, where] = (term + rs_r[k - 1, 1, where].astype(F32)).astype(BF)
            left = send(
                rs_s.at[k, 1, where], rs_r.at[k, 1, where],
                rss.at[gi, 2 * k + 3], rsr.at[gi, 2 * k + 3], down,
            )
        yield
        right.wait_recv()
        left.wait_recv()
        whole = part(g, 0) + rs_r[2, 0, where].astype(F32) + rs_r[2, 1, where].astype(F32)

        def rows(d):
            c = lax.rem(z + 8 + d, 8)
            return pl.ds(pl.multiple_of(l * 512 + c * 64, 64), 64)

        gram[where, rows(0), :] = (whole * (1.0 / 16384.0)).astype(BF)
        twins = []

        def to_twin(d, n):
            ref = gram.at[where, rows(d), :]
            twins.append(send(ref, ref, agps.at[gi, n], agpr.at[gi, n], twin))

        def hop(d, n, device, cols=slice(None)):
            ref = gram.at[where, rows(d), cols]
            return send(ref, ref, ags.at[gi, n], agr.at[gi, n], device)

        right = hop(0, 0, up)
        left = hop(0, 1, down)
        to_twin(0, 0)
        for k in range(1, 4):
            yield
            right.wait_recv()
            right = hop(-k, 2 * k, up, slice(None) if k < 3 else pl.ds(0, 128))
            to_twin(-k, 2 * k - 1)
            left.wait_recv()
            left = hop(k, 2 * k + 1, down, slice(None) if k < 3 else pl.ds(128, 128))
            to_twin(k, 2 * k)
        yield
        right.wait_recv()
        left.wait_recv()
        to_twin(4, 7)
        yield
        for copy in twins:
            copy.wait_recv()
        yield

    spmm(hbuf, hcg.at[x], 0, 4)
    xring = ring4x(hcg, x, 512, xs, xr, xr_dev, xl_dev)
    next(xring)
    spmm(hbuf, hcg.at[x], 4, 8)
    next(xring)
    next(yring)
    next(yring)
    own_s.wait()
    give_s.wait_recv()
    gram_part(0)
    spmm(sbuf, scg.at[y], 0, 8)
    sring = ring4(scg, y, 512, ss, sr, yr_dev, yl_dev)
    next(sring)
    next(sring)
    reducers = [z_reduce(gi) for gi in range(4)]

    def step(*which):
        for gi in which:
            next(reducers[gi])

    step(0)
    next(xring)
    step(0, 0)
    next(xring)
    step(0)
    next(xring)
    gram_part(1)
    step(0, 1, 0, 1)
    next(sring)
    next(xring)
    gram_part(2)
    gram_part(3)
    step(1, 2, 3, 0)
    for _ in range(2):
        step(1, 2, 3, 0)
    step(0)
    for _ in range(2):
        step(1, 2, 3)
    next(sring)
    next(sring)
    for _ in range(3):
        step(1, 2, 3)

    def project(p, i):
        total = jnp.zeros((512, 256), F32)
        for k in range(4):
            total += jnp.dot(
                scg[k, pl.ds(i * 512, 512), :], gram[p, k * 256 : (k + 1) * 256, :],
                preferred_element_type=F32,
            )
        return total

    opp_s[0] = project(1, 0).astype(BF)
    far_r = send(opp_s.at[0], opp_r.at[0], fs.at[0], fr.at[0], xr_dev)
    opp_s[1] = project(1, 1).astype(BF)
    far_l = send(opp_s.at[1], opp_r.at[1], fs.at[1], fr.at[1], xl_dev)
    step(2, 3)
    for i in range(2):
        own[i] = hcg[x, pl.ds(i * 512, 512), :].astype(F32) - project(0, i)
    step(2, 3)
    nb_s[0, 1] = project(2, 1).astype(BF)
    near = [send(nb_s.at[0, 1], nb_r.at[0, 1], fs.at[2], fr.at[2], xr_dev)]
    nb_s[1, 0] = project(3, 0).astype(BF)
    near.append(send(nb_s.at[1, 0], nb_r.at[1, 0], fs.at[3], fr.at[3], xl_dev))
    racc[0] = project(2, 0)
    racc[1] = project(3, 1)
    far_r.wait_recv()
    nb_s[0, 0] = (racc[0] + opp_r[0].astype(F32)).astype(BF)
    near.append(send(nb_s.at[0, 0], nb_r.at[0, 0], fs.at[4], fr.at[4], xr_dev))
    far_l.wait_recv()
    nb_s[1, 1] = (racc[1] + opp_r[1].astype(F32)).astype(BF)
    near.append(send(nb_s.at[1, 1], nb_r.at[1, 1], fs.at[5], fr.at[5], xl_dev))
    for copy in near:
        copy.wait_recv()
    for i in range(2):
        out[pl.ds(i * 512, 512), :] = own[i] - nb_r[0, i].astype(F32) - nb_r[1, i].astype(F32)
    for copy in sent:
        copy.wait_send()


def body(coeffs, block_sizes, neighbours, ham_blocks, ovl_blocks):
    vmem = pltpu.VMEM
    dma = pltpu.SemaphoreType.DMA
    n = len(GROUPS)
    smem = pl.BlockSpec(memory_space=pltpu.SMEM)
    hbm = pl.BlockSpec(memory_space=pl.ANY)
    return pl.pallas_call(
        kernel,
        out_shape=jax.ShapeDtypeStruct((1024, 256), F32),
        in_specs=[smem, smem, hbm, hbm, hbm],
        out_specs=pl.BlockSpec(memory_space=pltpu.VMEM),
        scratch_shapes=[
            vmem((2048, 256), BF),
            vmem((48, 128, 256), BF),
            vmem((8, 16, 128, 128), BF),
            vmem((8, 16, 128, 128), BF),
            vmem((4, 256, 1024), BF),
            vmem((4, 1024, 256), BF),
            vmem((4, 1024, 256), BF),
            vmem((4, 512, 256), F32),
            vmem((4, 512, 256), F32),
            vmem((4, 512, 256), F32),
            vmem((4, 1024, 256), BF),
            vmem((3, 2, 4, 64, 256), BF),
            vmem((3, 2, 4, 64, 256), BF),
            vmem((2, 4, 64, 128), BF),
            vmem((2, 4, 64, 128), BF),
            vmem((2, 512, 256), BF),
            vmem((2, 512, 256), BF),
            vmem((2, 2, 512, 256), BF),
            vmem((2, 2, 512, 256), BF),
            vmem((2, 512, 256), F32),
            vmem((2, 512, 256), F32),
            dma((3,)),
            dma((3,)), dma((3,)),
            dma((2,)), dma((2,)),
            dma((6,)), dma((6,)),
            dma((6,)), dma((6,)),
            dma((6,)), dma((6,)),
            dma((4,)), dma((4,)),
            dma((n, 8)), dma((n, 8)),
            dma((n, 8)), dma((n, 8)),
            dma((n, 8)), dma((n, 8)),
            dma((6,)), dma((6,)),
        ],
        compiler_params=pltpu.CompilerParams(
            collective_id=0, has_side_effects=True, vmem_limit_bytes=56 * 2**20
        ),
        cost_estimate=pl.CostEstimate(
            flops=6 * 2**30, bytes_accessed=12 * 2**20, transcendentals=0
        ),
        name="block_sparse_residual",
    )(block_sizes, neighbours, coeffs, ham_blocks, ovl_blocks)


def solution(mesh):
    return jax.shard_map(
        body,
        mesh=mesh,
        in_specs=(
            P("row", "col"),
            P("row"),
            P("row", None),
            P("row", "layer", None, None),
            P("row", "layer", None, None),
        ),
        out_specs=P(("row", "layer"), "col"),
        check_vma=False,
    )
```

```python
import jax
import jax.numpy as jnp
from jax import lax
from jax.experimental import pallas as pl
from jax.experimental.pallas import tpu as pltpu
from jax.sharding import PartitionSpec as P

MESH = pl.DeviceIdType.MESH
BF = jnp.bfloat16
F32 = jnp.float32
GROUPS = ((0,), (1,), (2,), (3,))


def kernel(
    sizes, neigh, coeffs, ham, ovl, out,
    raw, cbuf, hbuf, sbuf, ctg, hcg, scg, gown, gsend, grecv, gram,
    rs_s, rs_r, rs_s4, rs_r4, opp_s, opp_r, nb_s, nb_r, racc, own,
    loc, zs, zr, hs, hr, ys, yr, xs, xr, ss, sr, ps, pr,
    rss, rsr, ags, agr, agps, agpr, fs, fr,
):
    z = lax.axis_index("row")
    col = lax.axis_index("col")
    l = lax.axis_index("layer")
    x, y = col // 4, col % 4
    here = (z, col, l)
    up = (lax.rem(z + 1, 8), col, l)
    down = (lax.rem(z + 7, 8), col, l)
    up2 = (lax.rem(z + 2, 8), col, l)
    down2 = (lax.rem(z + 6, 8), col, l)
    xr_dev = (z, lax.rem(x + 1, 4) * 4 + y, l)
    xl_dev = (z, lax.rem(x + 3, 4) * 4 + y, l)
    yr_dev = (z, x * 4 + lax.rem(y + 1, 4), l)
    yl_dev = (z, x * 4 + lax.rem(y + 3, 4), l)
    twin = (z, col, 1 - l)
    del here

    def remote(src, dst, s, r, device):
        return pltpu.make_async_remote_copy(
            src_ref=src, dst_ref=dst, send_sem=s, recv_sem=r, device_id=device, device_id_type=MESH
        )

    sent = []

    def gone(copy):
        copy.wait_send()
        sent[:] = [other for other in sent if other is not copy]

    def send(src, dst, s, r, device):
        copy = remote(src, dst, s, r, device)
        copy.start()
        sent.append(copy)
        return copy

    load = pltpu.make_async_copy(coeffs, raw, loc.at[0])
    load.start()
    barrier = pltpu.get_barrier_semaphore()
    for device in (up, down, up2, down2, xr_dev, xl_dev, yr_dev, yl_dev, twin):
        pl.semaphore_signal(barrier, inc=1, device_id=device, device_id_type=MESH)
    own_h = pltpu.make_async_copy(
        ham.at[pl.ds(l * 8, 8)], hbuf.at[:, pl.ds(l * 8, 8)], loc.at[1]
    )
    own_s = pltpu.make_async_copy(
        ovl.at[pl.ds(l * 8, 8)], sbuf.at[:, pl.ds(l * 8, 8)], loc.at[2]
    )
    load.wait()

    def mask_block(b):
        block = raw[pl.ds(b * 128, 128), :].astype(F32)
        rows = lax.broadcasted_iota(jnp.int32, (128, 256), 0)
        cbuf[16 + b] = jnp.where(rows < sizes[b], block, 0.0).astype(BF)

    @pl.loop(0, 8)
    def _(i):
        mask_block(l * 8 + i)

    pl.semaphore_wait(barrier, 9)

    mine = cbuf.at[pl.ds(16 + l * 8, 8)]
    to_up = send(mine, cbuf.at[pl.ds(l * 8, 8)], zs.at[0], zr.at[0], up)
    to_down = send(mine, cbuf.at[pl.ds(32 + l * 8, 8)], zs.at[1], zr.at[1], down)
    give_h = send(
        ham.at[pl.ds((1 - l) * 8, 8)], hbuf.at[:, pl.ds(l * 8, 8)], hs.at[0], hr.at[0], twin
    )
    own_h.start()

    @pl.loop(0, 8)
    def _(i):
        ctg[y, :, pl.ds(pl.multiple_of(i * 128, 128), 128)] = cbuf[16 + l * 8 + i].T

    def ring4(buf, me, half, s, r, right, left):
        a, b = pl.ds(0, half), pl.ds(half, half)
        fa = lax.rem(me + 3, 4)
        fb = lax.rem(me + 1, 4)
        ra = send(buf.at[me, a], buf.at[me, a], s.at[0], r.at[0], right)
        lb = send(buf.at[me, b], buf.at[me, b], s.at[1], r.at[1], left)
        yield
        rb = send(buf.at[me, b], buf.at[me, b], s.at[2], r.at[2], right)
        la = send(buf.at[me, a], buf.at[me, a], s.at[3], r.at[3], left)
        yield
        ra.wait_recv()
        fra = send(buf.at[fa, a], buf.at[fa, a], s.at[4], r.at[4], right)
        lb.wait_recv()
        flb = send(buf.at[fb, b], buf.at[fb, b], s.at[5], r.at[5], left)
        yield
        rb.wait_recv()
        la.wait_recv()
        yield
        fra.wait_recv()
        flb.wait_recv()
        yield

    def ring4x(buf, me, half, s, r, right, left):
        a, b = pl.ds(0, half), pl.ds(half, half)
        fa = lax.rem(me + 3, 4)
        fb = lax.rem(me + 1, 4)
        ra = send(buf.at[me, a], buf.at[me, a], s.at[0], r.at[0], right)
        yield
        lb = send(buf.at[me, b], buf.at[me, b], s.at[1], r.at[1], left)
        yield
        ra.wait_recv()
        fra = send(buf.at[fa, a], buf.at[fa, a], s.at[2], r.at[2], right)
        lb.wait_recv()
        flb = send(buf.at[fb, b], buf.at[fb, b], s.at[3], r.at[3], left)
        yield
        gone(fra)
        rb = send(buf.at[me, b], buf.at[me, b], s.at[4], r.at[4], right)
        gone(flb)
        la = send(buf.at[me, a], buf.at[me, a], s.at[5], r.at[5], left)
        yield
        fra.wait_recv()
        flb.wait_recv()
        yield
        rb.wait_recv()
        la.wait_recv()
        yield

    yring = ring4(ctg, y, 128, ys, yr, yr_dev, yl_dev)
    next(yring)
    next(yring)
    give_s = send(
        ovl.at[pl.ds((1 - l) * 8, 8)], sbuf.at[:, pl.ds(l * 8, 8)], hs.at[1], hr.at[1], twin
    )
    own_s.start()

    @pl.loop(0, 8)
    def _(i):
        mask_block((1 - l) * 8 + i)

    next(yring)
    to_up.wait_recv()
    to_down.wait_recv()
    hand = jnp.where(l == 0, 32, 8)
    take = send(cbuf.at[pl.ds(hand, 8)], cbuf.at[pl.ds(hand, 8)], zs.at[2], zr.at[2], twin)
    own_h.wait()
    give_h.wait_recv()
    take.wait_recv()

    first = z * 16 - 16

    def picked(b, k):
        return cbuf[jnp.clip(neigh[b, k] - first, 0, 47)]

    def spmm(blocks, store, begin, end):
        @pl.loop(begin, end)
        def _(i):
            b = l * 8 + i
            total = jnp.zeros((128, 256), F32)
            for k in range(0, 16, 2):
                lhs = jnp.concatenate([blocks[i, k], blocks[i, k + 1]], axis=1)
                rhs = jnp.concatenate([picked(b, k), picked(b, k + 1)], axis=0)
                total += jnp.dot(lhs, rhs, preferred_element_type=F32)
            rows = lax.broadcasted_iota(jnp.int32, (128, 256), 0)
            store[pl.ds(pl.multiple_of(i * 128, 128), 128), :] = jnp.where(
                rows < sizes[b], total, 0.0
            ).astype(BF)

    slots = (x, lax.rem(x + 2, 4), lax.rem(x + 1, 4), lax.rem(x + 3, 4))
    swaps = {}

    def gram_part(p):
        rhs = hcg.at[slots[p]]

        @pl.loop(0, 2)
        def _(i):
            gsend[p, pl.ds(pl.multiple_of(i * 256, 256), 256), :] = jnp.dot(
                ctg[(1 - l) * 2 + i], rhs[...], preferred_element_type=F32
            )

        swaps[p] = send(gsend.at[p], grecv.at[p], ps.at[p], pr.at[p], twin)

        @pl.loop(0, 2)
        def _(i):
            gown[p, pl.ds(pl.multiple_of(i * 256, 256), 256), :] = jnp.dot(
                ctg[l * 2 + i], rhs[...], preferred_element_type=F32
            )

    def gram_add(p):
        swaps[p].wait_recv()
        gown[p] = gown[p] + grecv[p]

    def part(g, d):
        c = lax.rem(z + 8 + d, 8)
        return gown[g[0] : g[-1] + 1, pl.ds(pl.multiple_of(c * 64, 64), 64), :]

    def z_reduce(gi):
        g = GROUPS[gi]
        where = pl.ds(g[0], len(g))
        for p in g:
            gram_add(p)
        first = []
        for side, sign, one, two in ((0, 1, up, up2), (1, -1, down, down2)):
            rs_s[side, 0, where] = part(g, 3 * sign).astype(BF)
            rs_s4[side, where] = part(g, 4)[:, :, side * 128 : side * 128 + 128].astype(BF)
            n = 4 * side
            first.append((
                send(rs_s.at[side, 0, where], rs_r.at[side, 0, where], rss.at[gi, n], rsr.at[gi, n], one),
                send(rs_s4.at[side, where], rs_r4.at[side, where], rss.at[gi, n + 1], rsr.at[gi, n + 1], two),
            ))
        near = []
        for side, sign, one in ((0, 1, up), (1, -1, down)):
            rs_s[side, 1, where] = part(g, sign).astype(BF)
            n = 4 * side + 2
            near.append(send(
                rs_s.at[side, 1, where], rs_r.at[side, 1, where], rss.at[gi, n], rsr.at[gi, n], one
            ))
        yield
        for side, sign, two in ((0, 1, up2), (1, -1, down2)):
            three, four = first[side]
            lo, hi = side * 128, side * 128 + 128
            rest = slice(128, 256) if side == 0 else slice(0, 128)
            term = part(g, 2 * sign)
            three.wait_recv()
            four.wait_recv()
            term = term + rs_r[side, 0, where].astype(F32)
            rs_s[side, 2, where, :, lo:hi] = (
                term[:, :, lo:hi] + rs_r4[side, where].astype(F32)
            ).astype(BF)
            rs_s[side, 2, where, :, rest] = term[:, :, rest].astype(BF)
            n = 4 * side + 3
            near.append(send(
                rs_s.at[side, 2, where], rs_r.at[side, 2, where], rss.at[gi, n], rsr.at[gi, n], two
            ))
        yield
        whole = part(g, 0)
        for copy in near:
            copy.wait_recv()
        for side in range(2):
            whole = whole + rs_r[side, 1, where].astype(F32) + rs_r[side, 2, where].astype(F32)

        def rows(d):
            c = lax.rem(z + 8 + d, 8)
            return pl.ds(pl.multiple_of(l * 512 + c * 64, 64), 64)

        gram[where, rows(0), :] = (whole * (1.0 / 16384.0)).astype(BF)
        twins = []

        def to_twin(d, n):
            ref = gram.at[where, rows(d), :]
            twins.append(send(ref, ref, agps.at[gi, n], agpr.at[gi, n], twin))

        def hop(d, n, device, cols=slice(None)):
            ref = gram.at[where, rows(d), cols]
            return send(ref, ref, ags.at[gi, n], agr.at[gi, n], device)

        far = [hop(0, 0, up2), hop(0, 1, down2)]
        close = [hop(0, 2, up), hop(0, 3, down)]
        to_twin(0, 0)
        yield
        last = []
        for side, sign, one, two in ((0, -1, up, up2), (1, 1, down, down2)):
            far[side].wait_recv()
            last.append(hop(2 * sign, 4 + side, one))
            last.append(hop(2 * sign, 6 + side, two, pl.ds(side * 128, 128)))
        for side, sign in ((0, -1), (1, 1)):
            to_twin(2 * sign, 1 + side)
            close[side].wait_recv()
            to_twin(sign, 3 + side)
        yield
        for n, copy in enumerate(last):
            copy.wait_recv()
            if n % 2 == 0:
                to_twin(3 if n else -3, 5 + n // 2)
        to_twin(4, 7)
        yield
        for copy in twins:
            copy.wait_recv()
        yield

    spmm(hbuf, hcg.at[x], 0, 4)
    xring = ring4x(hcg, x, 512, xs, xr, xr_dev, xl_dev)
    next(xring)
    spmm(hbuf, hcg.at[x], 4, 8)
    next(xring)
    next(yring)
    next(yring)
    own_s.wait()
    give_s.wait_recv()
    gram_part(0)
    spmm(sbuf, scg.at[y], 0, 8)
    sring = ring4(scg, y, 512, ss, sr, yr_dev, yl_dev)
    next(sring)
    next(sring)
    reducers = [z_reduce(gi) for gi in range(4)]

    def step(*which):
        for gi in which:
            next(reducers[gi])

    step(0)
    next(xring)
    step(0, 0)
    next(xring)
    step(0)
    next(xring)
    gram_part(1)
    step(0, 1)
    next(sring)
    step(0, 1)
    next(xring)
    gram_part(2)
    gram_part(3)
    step(1, 2, 3)
    step(1, 2, 3)
    next(sring)
    next(sring)
    step(1, 2, 3)
    step(1)

    def project(p, i):
        total = jnp.zeros((512, 256), F32)
        for k in range(4):
            total += jnp.dot(
                scg[k, pl.ds(i * 512, 512), :], gram[p, k * 256 : (k + 1) * 256, :],
                preferred_element_type=F32,
            )
        return total

    opp_s[0] = project(1, 0).astype(BF)
    far_r = send(opp_s.at[0], opp_r.at[0], fs.at[0], fr.at[0], xr_dev)
    opp_s[1] = project(1, 1).astype(BF)
    far_l = send(opp_s.at[1], opp_r.at[1], fs.at[1], fr.at[1], xl_dev)
    step(2, 3)
    for i in range(2):
        own[i] = hcg[x, pl.ds(i * 512, 512), :].astype(F32) - project(0, i)
    step(2, 3)
    step(2, 3)
    nb_s[0, 1] = project(2, 1).astype(BF)
    near = [send(nb_s.at[0, 1], nb_r.at[0, 1], fs.at[2], fr.at[2], xr_dev)]
    nb_s[1, 0] = project(3, 0).astype(BF)
    near.append(send(nb_s.at[1, 0], nb_r.at[1, 0], fs.at[3], fr.at[3], xl_dev))
    racc[0] = project(2, 0)
    racc[1] = project(3, 1)
    far_r.wait_recv()
    nb_s[0, 0] = (racc[0] + opp_r[0].astype(F32)).astype(BF)
    near.append(send(nb_s.at[0, 0], nb_r.at[0, 0], fs.at[4], fr.at[4], xr_dev))
    far_l.wait_recv()
    nb_s[1, 1] = (racc[1] + opp_r[1].astype(F32)).astype(BF)
    near.append(send(nb_s.at[1, 1], nb_r.at[1, 1], fs.at[5], fr.at[5], xl_dev))
    for copy in near:
        copy.wait_recv()
    for i in range(2):
        out[pl.ds(i * 512, 512), :] = own[i] - nb_r[0, i].astype(F32) - nb_r[1, i].astype(F32)
    for copy in sent:
        copy.wait_send()


def body(coeffs, block_sizes, neighbours, ham_blocks, ovl_blocks):
    vmem = pltpu.VMEM
    dma = pltpu.SemaphoreType.DMA
    n = len(GROUPS)
    smem = pl.BlockSpec(memory_space=pltpu.SMEM)
    hbm = pl.BlockSpec(memory_space=pl.ANY)
    return pl.pallas_call(
        kernel,
        out_shape=jax.ShapeDtypeStruct((1024, 256), F32),
        in_specs=[smem, smem, hbm, hbm, hbm],
        out_specs=pl.BlockSpec(memory_space=pltpu.VMEM),
        scratch_shapes=[
            vmem((2048, 256), BF),
            vmem((48, 128, 256), BF),
            vmem((8, 16, 128, 128), BF),
            vmem((8, 16, 128, 128), BF),
            vmem((4, 256, 1024), BF),
            vmem((4, 1024, 256), BF),
            vmem((4, 1024, 256), BF),
            vmem((4, 512, 256), F32),
            vmem((4, 512, 256), F32),
            vmem((4, 512, 256), F32),
            vmem((4, 1024, 256), BF),
            vmem((2, 3, 4, 64, 256), BF),
            vmem((2, 3, 4, 64, 256), BF),
            vmem((2, 4, 64, 128), BF),
            vmem((2, 4, 64, 128), BF),
            vmem((2, 512, 256), BF),
            vmem((2, 512, 256), BF),
            vmem((2, 2, 512, 256), BF),
            vmem((2, 2, 512, 256), BF),
            vmem((2, 512, 256), F32),
            vmem((2, 512, 256), F32),
            dma((3,)),
            dma((3,)), dma((3,)),
            dma((2,)), dma((2,)),
            dma((6,)), dma((6,)),
            dma((6,)), dma((6,)),
            dma((6,)), dma((6,)),
            dma((4,)), dma((4,)),
            dma((n, 8)), dma((n, 8)),
            dma((n, 8)), dma((n, 8)),
            dma((n, 8)), dma((n, 8)),
            dma((6,)), dma((6,)),
        ],
        compiler_params=pltpu.CompilerParams(
            collective_id=0, has_side_effects=True, vmem_limit_bytes=56 * 2**20
        ),
        cost_estimate=pl.CostEstimate(
            flops=6 * 2**30, bytes_accessed=12 * 2**20, transcendentals=0
        ),
        name="block_sparse_residual",
    )(block_sizes, neighbours, coeffs, ham_blocks, ovl_blocks)


def solution(mesh):
    return jax.shard_map(
        body,
        mesh=mesh,
        in_specs=(
            P("row", "col"),
            P("row"),
            P("row", None),
            P("row", "layer", None, None),
            P("row", "layer", None, None),
        ),
        out_specs=P(("row", "layer"), "col"),
        check_vma=False,
    )
```

```python
import jax
import jax.numpy as jnp
from jax import lax
from jax.experimental import pallas as pl
from jax.experimental.pallas import tpu as pltpu
from jax.sharding import PartitionSpec as P

MESH = pl.DeviceIdType.MESH
BF = jnp.bfloat16
F32 = jnp.float32
GROUPS = ((0,), (1,), (2,), (3,))


def kernel(
    sizes, neigh, coeffs, ham, ovl, out,
    raw, cbuf, hbuf, sbuf, ctg, hcg, scg, gown, gsend, grecv, gram,
    rs_s, rs_r, rs_s4, rs_r4, opp_s, opp_r, nb_s, nb_r, racc, own,
    loc, zs, zr, hs, hr, ys, yr, xs, xr, ss, sr, ps, pr,
    rss, rsr, ags, agr, agps, agpr, fs, fr,
):
    z = lax.axis_index("row")
    col = lax.axis_index("col")
    l = lax.axis_index("layer")
    x, y = col // 4, col % 4
    here = (z, col, l)
    up = (lax.rem(z + 1, 8), col, l)
    down = (lax.rem(z + 7, 8), col, l)
    up2 = (lax.rem(z + 2, 8), col, l)
    down2 = (lax.rem(z + 6, 8), col, l)
    xr_dev = (z, lax.rem(x + 1, 4) * 4 + y, l)
    xl_dev = (z, lax.rem(x + 3, 4) * 4 + y, l)
    yr_dev = (z, x * 4 + lax.rem(y + 1, 4), l)
    yl_dev = (z, x * 4 + lax.rem(y + 3, 4), l)
    twin = (z, col, 1 - l)
    del here

    def remote(src, dst, s, r, device):
        return pltpu.make_async_remote_copy(
            src_ref=src, dst_ref=dst, send_sem=s, recv_sem=r, device_id=device, device_id_type=MESH
        )

    sent = []

    def send(src, dst, s, r, device):
        copy = remote(src, dst, s, r, device)
        copy.start()
        sent.append(copy)
        return copy

    load = pltpu.make_async_copy(coeffs, raw, loc.at[0])
    load.start()
    barrier = pltpu.get_barrier_semaphore()
    for device in (up, down, up2, down2, xr_dev, xl_dev, yr_dev, yl_dev, twin):
        pl.semaphore_signal(barrier, inc=1, device_id=device, device_id_type=MESH)
    own_h = pltpu.make_async_copy(
        ham.at[pl.ds(l * 8, 8)], hbuf.at[:, pl.ds(l * 8, 8)], loc.at[1]
    )
    own_s = pltpu.make_async_copy(
        ovl.at[pl.ds(l * 8, 8)], sbuf.at[:, pl.ds(l * 8, 8)], loc.at[2]
    )
    load.wait()

    def mask_block(b):
        block = raw[pl.ds(b * 128, 128), :].astype(F32)
        rows = lax.broadcasted_iota(jnp.int32, (128, 256), 0)
        cbuf[16 + b] = jnp.where(rows < sizes[b], block, 0.0).astype(BF)

    @pl.loop(0, 8)
    def _(i):
        mask_block(l * 8 + i)

    pl.semaphore_wait(barrier, 9)

    mine = cbuf.at[pl.ds(16 + l * 8, 8)]
    to_up = send(mine, cbuf.at[pl.ds(l * 8, 8)], zs.at[0], zr.at[0], up)
    to_down = send(mine, cbuf.at[pl.ds(32 + l * 8, 8)], zs.at[1], zr.at[1], down)
    give_h = send(
        ham.at[pl.ds((1 - l) * 8, 8)], hbuf.at[:, pl.ds(l * 8, 8)], hs.at[0], hr.at[0], twin
    )
    own_h.start()

    @pl.loop(0, 8)
    def _(i):
        ctg[y, :, pl.ds(pl.multiple_of(i * 128, 128), 128)] = cbuf[16 + l * 8 + i].T

    def ring4(buf, me, half, s, r, right, left):
        a, b = pl.ds(0, half), pl.ds(half, half)
        fa = lax.rem(me + 3, 4)
        fb = lax.rem(me + 1, 4)
        ra = send(buf.at[me, a], buf.at[me, a], s.at[0], r.at[0], right)
        lb = send(buf.at[me, b], buf.at[me, b], s.at[1], r.at[1], left)
        yield
        rb = send(buf.at[me, b], buf.at[me, b], s.at[2], r.at[2], right)
        la = send(buf.at[me, a], buf.at[me, a], s.at[3], r.at[3], left)
        yield
        ra.wait_recv()
        fra = send(buf.at[fa, a], buf.at[fa, a], s.at[4], r.at[4], right)
        lb.wait_recv()
        flb = send(buf.at[fb, b], buf.at[fb, b], s.at[5], r.at[5], left)
        yield
        rb.wait_recv()
        la.wait_recv()
        yield
        fra.wait_recv()
        flb.wait_recv()
        yield

    yring = ring4(ctg, y, 128, ys, yr, yr_dev, yl_dev)
    next(yring)
    next(yring)
    give_s = send(
        ovl.at[pl.ds((1 - l) * 8, 8)], sbuf.at[:, pl.ds(l * 8, 8)], hs.at[1], hr.at[1], twin
    )
    own_s.start()

    @pl.loop(0, 8)
    def _(i):
        mask_block((1 - l) * 8 + i)

    next(yring)
    to_up.wait_recv()
    to_down.wait_recv()
    hand = jnp.where(l == 0, 32, 8)
    take = send(cbuf.at[pl.ds(hand, 8)], cbuf.at[pl.ds(hand, 8)], zs.at[2], zr.at[2], twin)
    own_h.wait()
    give_h.wait_recv()
    take.wait_recv()

    first = z * 16 - 16

    def picked(b, k):
        return cbuf[jnp.clip(neigh[b, k] - first, 0, 47)]

    def spmm(blocks, store, begin, end):
        @pl.loop(begin, end)
        def _(i):
            b = l * 8 + i
            total = jnp.zeros((128, 256), F32)
            for k in range(0, 16, 2):
                lhs = jnp.concatenate([blocks[i, k], blocks[i, k + 1]], axis=1)
                rhs = jnp.concatenate([picked(b, k), picked(b, k + 1)], axis=0)
                total += jnp.dot(lhs, rhs, preferred_element_type=F32)
            rows = lax.broadcasted_iota(jnp.int32, (128, 256), 0)
            store[pl.ds(pl.multiple_of(i * 128, 128), 128), :] = jnp.where(
                rows < sizes[b], total, 0.0
            ).astype(BF)

    slots = (x, lax.rem(x + 2, 4), lax.rem(x + 1, 4), lax.rem(x + 3, 4))
    swaps = {}

    def gram_part(p):
        rhs = hcg.at[slots[p]]

        @pl.loop(0, 2)
        def _(i):
            gsend[p, pl.ds(pl.multiple_of(i * 256, 256), 256), :] = jnp.dot(
                ctg[(1 - l) * 2 + i], rhs[...], preferred_element_type=F32
            )

        swaps[p] = send(gsend.at[p], grecv.at[p], ps.at[p], pr.at[p], twin)

        @pl.loop(0, 2)
        def _(i):
            gown[p, pl.ds(pl.multiple_of(i * 256, 256), 256), :] = jnp.dot(
                ctg[l * 2 + i], rhs[...], preferred_element_type=F32
            )

    def gram_add(p):
        swaps[p].wait_recv()
        gown[p] = gown[p] + grecv[p]

    def part(g, d):
        c = lax.rem(z + 8 + d, 8)
        return gown[g[0] : g[-1] + 1, pl.ds(pl.multiple_of(c * 64, 64), 64), :]

    def z_reduce(gi):
        g = GROUPS[gi]
        where = pl.ds(g[0], len(g))
        for p in g:
            gram_add(p)
        first = []
        for side, sign, one, two in ((0, 1, up, up2), (1, -1, down, down2)):
            rs_s[side, 0, where] = part(g, 3 * sign).astype(BF)
            rs_s4[side, where] = part(g, 4)[:, :, side * 128 : side * 128 + 128].astype(BF)
            n = 4 * side
            first.append((
                send(rs_s.at[side, 0, where], rs_r.at[side, 0, where], rss.at[gi, n], rsr.at[gi, n], one),
                send(rs_s4.at[side, where], rs_r4.at[side, where], rss.at[gi, n + 1], rsr.at[gi, n + 1], two),
            ))
        near = []
        for side, sign, one in ((0, 1, up), (1, -1, down)):
            rs_s[side, 1, where] = part(g, sign).astype(BF)
            n = 4 * side + 2
            near.append(send(
                rs_s.at[side, 1, where], rs_r.at[side, 1, where], rss.at[gi, n], rsr.at[gi, n], one
            ))
        yield
        for side, sign, two in ((0, 1, up2), (1, -1, down2)):
            three, four = first[side]
            lo, hi = side * 128, side * 128 + 128
            rest = slice(128, 256) if side == 0 else slice(0, 128)
            term = part(g, 2 * sign)
            three.wait_recv()
            four.wait_recv()
            term = term + rs_r[side, 0, where].astype(F32)
            rs_s[side, 2, where, :, lo:hi] = (
                term[:, :, lo:hi] + rs_r4[side, where].astype(F32)
            ).astype(BF)
            rs_s[side, 2, where, :, rest] = term[:, :, rest].astype(BF)
            n = 4 * side + 3
            near.append(send(
                rs_s.at[side, 2, where], rs_r.at[side, 2, where], rss.at[gi, n], rsr.at[gi, n], two
            ))
        yield
        whole = part(g, 0)
        for copy in near:
            copy.wait_recv()
        for side in range(2):
            whole = whole + rs_r[side, 1, where].astype(F32) + rs_r[side, 2, where].astype(F32)

        def rows(d):
            c = lax.rem(z + 8 + d, 8)
            return pl.ds(pl.multiple_of(l * 512 + c * 64, 64), 64)

        gram[where, rows(0), :] = (whole * (1.0 / 16384.0)).astype(BF)
        twins = []

        def to_twin(d, n):
            ref = gram.at[where, rows(d), :]
            twins.append(send(ref, ref, agps.at[gi, n], agpr.at[gi, n], twin))

        def hop(d, n, device, cols=slice(None)):
            ref = gram.at[where, rows(d), cols]
            return send(ref, ref, ags.at[gi, n], agr.at[gi, n], device)

        far = [hop(0, 0, up2), hop(0, 1, down2)]
        close = [hop(0, 2, up), hop(0, 3, down)]
        to_twin(0, 0)
        yield
        last = []
        for side, sign, one, two in ((0, -1, up, up2), (1, 1, down, down2)):
            far[side].wait_recv()
            last.append(hop(2 * sign, 4 + side, one))
            last.append(hop(2 * sign, 6 + side, two, pl.ds(side * 128, 128)))
        for side, sign in ((0, -1), (1, 1)):
            to_twin(2 * sign, 1 + side)
            close[side].wait_recv()
            to_twin(sign, 3 + side)
        yield
        for n, copy in enumerate(last):
            copy.wait_recv()
            if n % 2 == 0:
                to_twin(3 if n else -3, 5 + n // 2)
        to_twin(4, 7)
        yield
        for copy in twins:
            copy.wait_recv()
        yield

    spmm(hbuf, hcg.at[x], 0, 8)
    xring = ring4(hcg, x, 512, xs, xr, xr_dev, xl_dev)
    next(xring)
    next(xring)
    next(yring)
    next(yring)
    own_s.wait()
    give_s.wait_recv()
    gram_part(0)
    spmm(sbuf, scg.at[y], 0, 8)
    sring = ring4(scg, y, 512, ss, sr, yr_dev, yl_dev)
    next(sring)
    next(sring)
    reducers = [z_reduce(gi) for gi in range(4)]

    def step(*which):
        for gi in which:
            next(reducers[gi])

    step(0)
    step(0)
    next(xring)
    next(xring)
    gram_part(2)
    gram_part(3)
    step(0)
    step(2, 3)
    next(sring)
    step(0)
    step(2, 3)
    next(xring)
    gram_part(1)
    step(2, 3)
    step(1)
    step(0)
    step(2, 3)
    step(1)
    step(0)
    step(2, 3)
    step(1)
    next(sring)
    next(sring)
    step(2, 3)

    def project(p, i):
        total = jnp.zeros((512, 256), F32)
        for k in range(4):
            total += jnp.dot(
                scg[k, pl.ds(i * 512, 512), :], gram[p, k * 256 : (k + 1) * 256, :],
                preferred_element_type=F32,
            )
        return total

    nb_s[0, 1] = project(2, 1).astype(BF)
    near = [send(nb_s.at[0, 1], nb_r.at[0, 1], fs.at[2], fr.at[2], xr_dev)]
    nb_s[1, 0] = project(3, 0).astype(BF)
    near.append(send(nb_s.at[1, 0], nb_r.at[1, 0], fs.at[3], fr.at[3], xl_dev))
    step(1)
    racc[0] = project(2, 0)
    racc[1] = project(3, 1)
    step(1)
    step(1)
    opp_s[0] = project(1, 0).astype(BF)
    far_r = send(opp_s.at[0], opp_r.at[0], fs.at[0], fr.at[0], xr_dev)
    opp_s[1] = project(1, 1).astype(BF)
    far_l = send(opp_s.at[1], opp_r.at[1], fs.at[1], fr.at[1], xl_dev)
    for i in range(2):
        own[i] = hcg[x, pl.ds(i * 512, 512), :].astype(F32) - project(0, i)
    far_r.wait_recv()
    nb_s[0, 0] = (racc[0] + opp_r[0].astype(F32)).astype(BF)
    near.append(send(nb_s.at[0, 0], nb_r.at[0, 0], fs.at[4], fr.at[4], xr_dev))
    far_l.wait_recv()
    nb_s[1, 1] = (racc[1] + opp_r[1].astype(F32)).astype(BF)
    near.append(send(nb_s.at[1, 1], nb_r.at[1, 1], fs.at[5], fr.at[5], xl_dev))
    for copy in near:
        copy.wait_recv()
    for i in range(2):
        out[pl.ds(i * 512, 512), :] = own[i] - nb_r[0, i].astype(F32) - nb_r[1, i].astype(F32)
    for copy in sent:
        copy.wait_send()


def body(coeffs, block_sizes, neighbours, ham_blocks, ovl_blocks):
    vmem = pltpu.VMEM
    dma = pltpu.SemaphoreType.DMA
    n = len(GROUPS)
    smem = pl.BlockSpec(memory_space=pltpu.SMEM)
    hbm = pl.BlockSpec(memory_space=pl.ANY)
    return pl.pallas_call(
        kernel,
        out_shape=jax.ShapeDtypeStruct((1024, 256), F32),
        in_specs=[smem, smem, hbm, hbm, hbm],
        out_specs=pl.BlockSpec(memory_space=pltpu.VMEM),
        scratch_shapes=[
            vmem((2048, 256), BF),
            vmem((48, 128, 256), BF),
            vmem((8, 16, 128, 128), BF),
            vmem((8, 16, 128, 128), BF),
            vmem((4, 256, 1024), BF),
            vmem((4, 1024, 256), BF),
            vmem((4, 1024, 256), BF),
            vmem((4, 512, 256), F32),
            vmem((4, 512, 256), F32),
            vmem((4, 512, 256), F32),
            vmem((4, 1024, 256), BF),
            vmem((2, 3, 4, 64, 256), BF),
            vmem((2, 3, 4, 64, 256), BF),
            vmem((2, 4, 64, 128), BF),
            vmem((2, 4, 64, 128), BF),
            vmem((2, 512, 256), BF),
            vmem((2, 512, 256), BF),
            vmem((2, 2, 512, 256), BF),
            vmem((2, 2, 512, 256), BF),
            vmem((2, 512, 256), F32),
            vmem((2, 512, 256), F32),
            dma((3,)),
            dma((3,)), dma((3,)),
            dma((2,)), dma((2,)),
            dma((6,)), dma((6,)),
            dma((6,)), dma((6,)),
            dma((6,)), dma((6,)),
            dma((4,)), dma((4,)),
            dma((n, 8)), dma((n, 8)),
            dma((n, 8)), dma((n, 8)),
            dma((n, 8)), dma((n, 8)),
            dma((6,)), dma((6,)),
        ],
        compiler_params=pltpu.CompilerParams(
            collective_id=0, has_side_effects=True, vmem_limit_bytes=56 * 2**20
        ),
        cost_estimate=pl.CostEstimate(
            flops=6 * 2**30, bytes_accessed=12 * 2**20, transcendentals=0
        ),
        name="block_sparse_residual",
    )(block_sizes, neighbours, coeffs, ham_blocks, ovl_blocks)


def solution(mesh):
    return jax.shard_map(
        body,
        mesh=mesh,
        in_specs=(
            P("row", "col"),
            P("row"),
            P("row", None),
            P("row", "layer", None, None),
            P("row", "layer", None, None),
        ),
        out_specs=P(("row", "layer"), "col"),
        check_vma=False,
    )
```

```python
import jax
import jax.numpy as jnp
from jax import lax
from jax.experimental import pallas as pl
from jax.experimental.pallas import tpu as pltpu
from jax.sharding import PartitionSpec as P

MESH = pl.DeviceIdType.MESH
BF = jnp.bfloat16
F32 = jnp.float32
GROUPS = ((0,), (1,), (2,), (3,))


def kernel(
    sizes, neigh, coeffs, ham, ovl, out,
    raw, cbuf, hbuf, sbuf, ctg, hcg, scg, gown, gsend, grecv, gram,
    rs_s, rs_r, rs_s4, rs_r4, opp_s, opp_r, nb_s, nb_r, racc, own,
    loc, zs, zr, hs, hr, ys, yr, xs, xr, ss, sr, ps, pr,
    rss, rsr, ags, agr, agps, agpr, fs, fr,
):
    z = lax.axis_index("row")
    col = lax.axis_index("col")
    l = lax.axis_index("layer")
    x, y = col // 4, col % 4
    here = (z, col, l)
    up = (lax.rem(z + 1, 8), col, l)
    down = (lax.rem(z + 7, 8), col, l)
    up2 = (lax.rem(z + 2, 8), col, l)
    down2 = (lax.rem(z + 6, 8), col, l)
    xr_dev = (z, lax.rem(x + 1, 4) * 4 + y, l)
    xl_dev = (z, lax.rem(x + 3, 4) * 4 + y, l)
    yr_dev = (z, x * 4 + lax.rem(y + 1, 4), l)
    yl_dev = (z, x * 4 + lax.rem(y + 3, 4), l)
    twin = (z, col, 1 - l)
    del here

    def remote(src, dst, s, r, device):
        return pltpu.make_async_remote_copy(
            src_ref=src, dst_ref=dst, send_sem=s, recv_sem=r, device_id=device, device_id_type=MESH
        )

    sent = []

    def send(src, dst, s, r, device):
        copy = remote(src, dst, s, r, device)
        copy.start()
        sent.append(copy)
        return copy

    load = pltpu.make_async_copy(coeffs, raw, loc.at[0])
    load.start()
    barrier = pltpu.get_barrier_semaphore()
    for device in (up, down, up2, down2, xr_dev, xl_dev, yr_dev, yl_dev, twin):
        pl.semaphore_signal(barrier, inc=1, device_id=device, device_id_type=MESH)
    own_h = pltpu.make_async_copy(
        ham.at[pl.ds(l * 8, 8)], hbuf.at[:, pl.ds(l * 8, 8)], loc.at[1]
    )
    own_s = pltpu.make_async_copy(
        ovl.at[pl.ds(l * 8, 8)], sbuf.at[:, pl.ds(l * 8, 8)], loc.at[2]
    )
    load.wait()

    def mask_block(b):
        block = raw[pl.ds(b * 128, 128), :].astype(F32)
        rows = lax.broadcasted_iota(jnp.int32, (128, 256), 0)
        cbuf[16 + b] = jnp.where(rows < sizes[b], block, 0.0).astype(BF)

    @pl.loop(0, 8)
    def _(i):
        mask_block(l * 8 + i)

    pl.semaphore_wait(barrier, 9)

    mine = cbuf.at[pl.ds(16 + l * 8, 8)]
    to_up = send(mine, cbuf.at[pl.ds(l * 8, 8)], zs.at[0], zr.at[0], up)
    to_down = send(mine, cbuf.at[pl.ds(32 + l * 8, 8)], zs.at[1], zr.at[1], down)
    give_h = send(
        ham.at[pl.ds((1 - l) * 8, 8)], hbuf.at[:, pl.ds(l * 8, 8)], hs.at[0], hr.at[0], twin
    )
    own_h.start()

    @pl.loop(0, 8)
    def _(i):
        ctg[y, :, pl.ds(pl.multiple_of(i * 128, 128), 128)] = cbuf[16 + l * 8 + i].T

    def ring4(buf, me, half, s, r, right, left):
        a, b = pl.ds(0, half), pl.ds(half, half)
        fa = lax.rem(me + 3, 4)
        fb = lax.rem(me + 1, 4)
        ra = send(buf.at[me, a], buf.at[me, a], s.at[0], r.at[0], right)
        lb = send(buf.at[me, b], buf.at[me, b], s.at[1], r.at[1], left)
        yield
        rb = send(buf.at[me, b], buf.at[me, b], s.at[2], r.at[2], right)
        la = send(buf.at[me, a], buf.at[me, a], s.at[3], r.at[3], left)
        yield
        ra.wait_recv()
        fra = send(buf.at[fa, a], buf.at[fa, a], s.at[4], r.at[4], right)
        lb.wait_recv()
        flb = send(buf.at[fb, b], buf.at[fb, b], s.at[5], r.at[5], left)
        yield
        rb.wait_recv()
        la.wait_recv()
        yield
        fra.wait_recv()
        flb.wait_recv()
        yield

    yring = ring4(ctg, y, 128, ys, yr, yr_dev, yl_dev)
    next(yring)
    next(yring)
    give_s = send(
        ovl.at[pl.ds((1 - l) * 8, 8)], sbuf.at[:, pl.ds(l * 8, 8)], hs.at[1], hr.at[1], twin
    )
    own_s.start()

    @pl.loop(0, 8)
    def _(i):
        mask_block((1 - l) * 8 + i)

    next(yring)
    to_up.wait_recv()
    to_down.wait_recv()
    hand = jnp.where(l == 0, 32, 8)
    take = send(cbuf.at[pl.ds(hand, 8)], cbuf.at[pl.ds(hand, 8)], zs.at[2], zr.at[2], twin)
    own_h.wait()
    give_h.wait_recv()
    take.wait_recv()

    first = z * 16 - 16

    def picked(b, k):
        return cbuf[jnp.clip(neigh[b, k] - first, 0, 47)]

    def spmm(blocks, store, begin, end):
        @pl.loop(begin, end)
        def _(i):
            b = l * 8 + i
            total = jnp.zeros((128, 256), F32)
            for k in range(0, 16, 2):
                lhs = jnp.concatenate([blocks[i, k], blocks[i, k + 1]], axis=1)
                rhs = jnp.concatenate([picked(b, k), picked(b, k + 1)], axis=0)
                total += jnp.dot(lhs, rhs, preferred_element_type=F32)
            rows = lax.broadcasted_iota(jnp.int32, (128, 256), 0)
            store[pl.ds(pl.multiple_of(i * 128, 128), 128), :] = jnp.where(
                rows < sizes[b], total, 0.0
            ).astype(BF)

    slots = (x, lax.rem(x + 2, 4), lax.rem(x + 1, 4), lax.rem(x + 3, 4))
    swaps = {}

    def gram_part(p):
        rhs = hcg.at[slots[p]]

        @pl.loop(0, 2)
        def _(i):
            gsend[p, pl.ds(pl.multiple_of(i * 256, 256), 256), :] = jnp.dot(
                ctg[(1 - l) * 2 + i], rhs[...], preferred_element_type=F32
            )

        swaps[p] = send(gsend.at[p], grecv.at[p], ps.at[p], pr.at[p], twin)

        @pl.loop(0, 2)
        def _(i):
            gown[p, pl.ds(pl.multiple_of(i * 256, 256), 256), :] = jnp.dot(
                ctg[l * 2 + i], rhs[...], preferred_element_type=F32
            )

    def gram_add(p):
        swaps[p].wait_recv()
        gown[p] = gown[p] + grecv[p]

    def part(g, d):
        c = lax.rem(z + 8 + d, 8)
        return gown[g[0] : g[-1] + 1, pl.ds(pl.multiple_of(c * 64, 64), 64), :]

    def z_reduce(gi):
        g = GROUPS[gi]
        where = pl.ds(g[0], len(g))
        for p in g:
            gram_add(p)
        first = []
        for side, sign, one, two in ((0, 1, up, up2), (1, -1, down, down2)):
            rs_s[side, 0, where] = part(g, 3 * sign).astype(BF)
            rs_s4[side, where] = part(g, 4)[:, :, side * 128 : side * 128 + 128].astype(BF)
            n = 4 * side
            first.append((
                send(rs_s.at[side, 0, where], rs_r.at[side, 0, where], rss.at[gi, n], rsr.at[gi, n], one),
                send(rs_s4.at[side, where], rs_r4.at[side, where], rss.at[gi, n + 1], rsr.at[gi, n + 1], two),
            ))
        near = []
        for side, sign, one in ((0, 1, up), (1, -1, down)):
            rs_s[side, 1, where] = part(g, sign).astype(BF)
            n = 4 * side + 2
            near.append(send(
                rs_s.at[side, 1, where], rs_r.at[side, 1, where], rss.at[gi, n], rsr.at[gi, n], one
            ))
        yield
        for side, sign, two in ((0, 1, up2), (1, -1, down2)):
            three, four = first[side]
            lo, hi = side * 128, side * 128 + 128
            rest = slice(128, 256) if side == 0 else slice(0, 128)
            term = part(g, 2 * sign)
            three.wait_recv()
            four.wait_recv()
            term = term + rs_r[side, 0, where].astype(F32)
            rs_s[side, 2, where, :, lo:hi] = (
                term[:, :, lo:hi] + rs_r4[side, where].astype(F32)
            ).astype(BF)
            rs_s[side, 2, where, :, rest] = term[:, :, rest].astype(BF)
            n = 4 * side + 3
            near.append(send(
                rs_s.at[side, 2, where], rs_r.at[side, 2, where], rss.at[gi, n], rsr.at[gi, n], two
            ))
        yield
        whole = part(g, 0)
        for copy in near:
            copy.wait_recv()
        for side in range(2):
            whole = whole + rs_r[side, 1, where].astype(F32) + rs_r[side, 2, where].astype(F32)

        def rows(d):
            c = lax.rem(z + 8 + d, 8)
            return pl.ds(pl.multiple_of(l * 512 + c * 64, 64), 64)

        gram[where, rows(0), :] = (whole * (1.0 / 16384.0)).astype(BF)
        twins = []

        def to_twin(d, n):
            ref = gram.at[where, rows(d), :]
            twins.append(send(ref, ref, agps.at[gi, n], agpr.at[gi, n], twin))

        def hop(d, n, device, cols=slice(None)):
            ref = gram.at[where, rows(d), cols]
            return send(ref, ref, ags.at[gi, n], agr.at[gi, n], device)

        far = [hop(0, 0, up2), hop(0, 1, down2)]
        close = [hop(0, 2, up), hop(0, 3, down)]
        to_twin(0, 0)
        yield
        last = []
        for side, sign, one, two in ((0, -1, up, up2), (1, 1, down, down2)):
            far[side].wait_recv()
            last.append(hop(2 * sign, 4 + side, one))
            last.append(hop(2 * sign, 6 + side, two, pl.ds(side * 128, 128)))
        for side, sign in ((0, -1), (1, 1)):
            to_twin(2 * sign, 1 + side)
            close[side].wait_recv()
            to_twin(sign, 3 + side)
        yield
        for n, copy in enumerate(last):
            copy.wait_recv()
            if n % 2 == 0:
                to_twin(3 if n else -3, 5 + n // 2)
        to_twin(4, 7)
        yield
        for copy in twins:
            copy.wait_recv()
        yield

    spmm(hbuf, hcg.at[x], 0, 8)
    xring = ring4(hcg, x, 512, xs, xr, xr_dev, xl_dev)
    next(xring)
    next(xring)
    next(yring)
    next(yring)
    own_s.wait()
    give_s.wait_recv()
    gram_part(0)
    spmm(sbuf, scg.at[y], 0, 8)
    sring = ring4(scg, y, 512, ss, sr, yr_dev, yl_dev)
    next(sring)
    next(sring)
    reducers = [z_reduce(gi) for gi in range(4)]

    def step(*which):
        for gi in which:
            next(reducers[gi])

    step(0)
    step(0)
    next(xring)
    next(xring)
    gram_part(2)
    gram_part(3)
    step(0)
    step(2, 3)
    next(sring)
    step(0)
    step(2, 3)
    next(xring)
    gram_part(1)
    step(2, 3)
    step(1)
    step(0)
    step(2, 3)
    step(1)
    step(0)
    step(2, 3)
    step(1)
    next(sring)
    next(sring)
    step(2, 3)

    def project(p, i):
        total = jnp.zeros((512, 256), F32)
        for k in range(4):
            total += jnp.dot(
                scg[k, pl.ds(i * 512, 512), :], gram[p, k * 256 : (k + 1) * 256, :],
                preferred_element_type=F32,
            )
        return total

    nb_s[0, 1] = project(2, 1).astype(BF)
    near = [send(nb_s.at[0, 1], nb_r.at[0, 1], fs.at[4], fr.at[4], xr_dev)]
    nb_s[1, 0] = project(3, 0).astype(BF)
    near.append(send(nb_s.at[1, 0], nb_r.at[1, 0], fs.at[5], fr.at[5], xl_dev))
    step(1)
    racc[0] = project(2, 0)
    racc[1] = project(3, 1)
    step(1)
    step(1)
    pieces = (pl.ds(0, 256), pl.ds(256, 256))
    far = []
    for side, device in ((0, xr_dev), (1, xl_dev)):
        opp_s[side] = project(1, side).astype(BF)
        for q, rows in enumerate(pieces):
            n = 2 * q + side
            far.append(send(opp_s.at[side, rows], opp_r.at[side, rows], fs.at[n], fr.at[n], device))
    for i in range(2):
        own[i] = hcg[x, pl.ds(i * 512, 512), :].astype(F32) - project(0, i)
    for q, rows in enumerate(pieces):
        for side, device in ((0, xr_dev), (1, xl_dev)):
            far[2 * side + q].wait_recv()
            nb_s[side, side, rows] = (racc[side, rows] + opp_r[side, rows].astype(F32)).astype(BF)
            n = 6 + 2 * q + side
            near.append(send(
                nb_s.at[side, side, rows], nb_r.at[side, side, rows], fs.at[n], fr.at[n], device
            ))
    for copy in near:
        copy.wait_recv()
    for i in range(2):
        out[pl.ds(i * 512, 512), :] = own[i] - nb_r[0, i].astype(F32) - nb_r[1, i].astype(F32)
    for copy in sent:
        copy.wait_send()


def body(coeffs, block_sizes, neighbours, ham_blocks, ovl_blocks):
    vmem = pltpu.VMEM
    dma = pltpu.SemaphoreType.DMA
    n = len(GROUPS)
    smem = pl.BlockSpec(memory_space=pltpu.SMEM)
    hbm = pl.BlockSpec(memory_space=pl.ANY)
    return pl.pallas_call(
        kernel,
        out_shape=jax.ShapeDtypeStruct((1024, 256), F32),
        in_specs=[smem, smem, hbm, hbm, hbm],
        out_specs=pl.BlockSpec(memory_space=pltpu.VMEM),
        scratch_shapes=[
            vmem((2048, 256), BF),
            vmem((48, 128, 256), BF),
            vmem((8, 16, 128, 128), BF),
            vmem((8, 16, 128, 128), BF),
            vmem((4, 256, 1024), BF),
            vmem((4, 1024, 256), BF),
            vmem((4, 1024, 256), BF),
            vmem((4, 512, 256), F32),
            vmem((4, 512, 256), F32),
            vmem((4, 512, 256), F32),
            vmem((4, 1024, 256), BF),
            vmem((2, 3, 4, 64, 256), BF),
            vmem((2, 3, 4, 64, 256), BF),
            vmem((2, 4, 64, 128), BF),
            vmem((2, 4, 64, 128), BF),
            vmem((2, 512, 256), BF),
            vmem((2, 512, 256), BF),
            vmem((2, 2, 512, 256), BF),
            vmem((2, 2, 512, 256), BF),
            vmem((2, 512, 256), F32),
            vmem((2, 512, 256), F32),
            dma((3,)),
            dma((3,)), dma((3,)),
            dma((2,)), dma((2,)),
            dma((6,)), dma((6,)),
            dma((6,)), dma((6,)),
            dma((6,)), dma((6,)),
            dma((4,)), dma((4,)),
            dma((n, 8)), dma((n, 8)),
            dma((n, 8)), dma((n, 8)),
            dma((n, 8)), dma((n, 8)),
            dma((10,)), dma((10,)),
        ],
        compiler_params=pltpu.CompilerParams(
            collective_id=0, has_side_effects=True, vmem_limit_bytes=56 * 2**20
        ),
        cost_estimate=pl.CostEstimate(
            flops=6 * 2**30, bytes_accessed=12 * 2**20, transcendentals=0
        ),
        name="block_sparse_residual",
    )(block_sizes, neighbours, coeffs, ham_blocks, ovl_blocks)


def solution(mesh):
    return jax.shard_map(
        body,
        mesh=mesh,
        in_specs=(
            P("row", "col"),
            P("row"),
            P("row", None),
            P("row", "layer", None, None),
            P("row", "layer", None, None),
        ),
        out_specs=P(("row", "layer"), "col"),
        check_vma=False,
    )
```

```python
import jax
import jax.numpy as jnp
from jax import lax
from jax.experimental import pallas as pl
from jax.experimental.pallas import tpu as pltpu
from jax.sharding import PartitionSpec as P

MESH = pl.DeviceIdType.MESH
BF = jnp.bfloat16
F32 = jnp.float32
GROUPS = ((0,), (1,), (2,), (3,))


def kernel(
    sizes, neigh, coeffs, ham, ovl, out,
    raw, cbuf, hbuf, sbuf, ctg, hcg, scg, gown, gsend, grecv, gram,
    rs_s, rs_r, rs_s4, rs_r4, opp_s, opp_r, nb_s, nb_r, racc, own,
    loc, zs, zr, hs, hr, ys, yr, xs, xr, ss, sr, ps, pr,
    rss, rsr, ags, agr, agps, agpr, fs, fr,
):
    z = lax.axis_index("row")
    col = lax.axis_index("col")
    l = lax.axis_index("layer")
    x, y = col // 4, col % 4
    here = (z, col, l)
    up = (lax.rem(z + 1, 8), col, l)
    down = (lax.rem(z + 7, 8), col, l)
    up2 = (lax.rem(z + 2, 8), col, l)
    down2 = (lax.rem(z + 6, 8), col, l)
    xr_dev = (z, lax.rem(x + 1, 4) * 4 + y, l)
    xl_dev = (z, lax.rem(x + 3, 4) * 4 + y, l)
    yr_dev = (z, x * 4 + lax.rem(y + 1, 4), l)
    yl_dev = (z, x * 4 + lax.rem(y + 3, 4), l)
    twin = (z, col, 1 - l)
    del here

    def remote(src, dst, s, r, device):
        return pltpu.make_async_remote_copy(
            src_ref=src, dst_ref=dst, send_sem=s, recv_sem=r, device_id=device, device_id_type=MESH
        )

    sent = []

    def send(src, dst, s, r, device):
        copy = remote(src, dst, s, r, device)
        copy.start()
        sent.append(copy)
        return copy

    load = pltpu.make_async_copy(coeffs, raw, loc.at[0])
    load.start()
    barrier = pltpu.get_barrier_semaphore()
    for device in (up, down, up2, down2, xr_dev, xl_dev, yr_dev, yl_dev, twin):
        pl.semaphore_signal(barrier, inc=1, device_id=device, device_id_type=MESH)
    own_h = pltpu.make_async_copy(
        ham.at[pl.ds(l * 8, 8)], hbuf.at[:, pl.ds(l * 8, 8)], loc.at[1]
    )
    own_s = pltpu.make_async_copy(
        ovl.at[pl.ds(l * 8, 8)], sbuf.at[:, pl.ds(l * 8, 8)], loc.at[2]
    )
    load.wait()

    def mask_block(b):
        block = raw[pl.ds(b * 128, 128), :].astype(F32)
        rows = lax.broadcasted_iota(jnp.int32, (128, 256), 0)
        cbuf[16 + b] = jnp.where(rows < sizes[b], block, 0.0).astype(BF)

    @pl.loop(0, 8)
    def _(i):
        mask_block(l * 8 + i)

    pl.semaphore_wait(barrier, 9)

    halo = []
    for q in range(2):
        mine = cbuf.at[pl.ds(16 + l * 8 + 4 * q, 4)]
        halo.append((
            send(mine, cbuf.at[pl.ds(l * 8 + 4 * q, 4)], zs.at[3 * q], zr.at[3 * q], up),
            send(mine, cbuf.at[pl.ds(32 + l * 8 + 4 * q, 4)], zs.at[3 * q + 1], zr.at[3 * q + 1], down),
        ))
    give_h = send(
        ham.at[pl.ds((1 - l) * 8, 8)], hbuf.at[:, pl.ds(l * 8, 8)], hs.at[0], hr.at[0], twin
    )
    own_h.start()

    @pl.loop(0, 8)
    def _(i):
        ctg[y, :, pl.ds(pl.multiple_of(i * 128, 128), 128)] = cbuf[16 + l * 8 + i].T

    def ring4(buf, me, half, s, r, right, left, pieces=1):
        a, b = pl.ds(0, half), pl.ds(half, half)
        fa = lax.rem(me + 3, 4)
        fb = lax.rem(me + 1, 4)
        size = half // pieces
        lows = [pl.ds(q * size, size) for q in range(pieces)]
        highs = [pl.ds(half + q * size, size) for q in range(pieces)]

        def go(slot, rows, n, device):
            ref = buf.at[slot, rows]
            return send(ref, ref, s.at[n], r.at[n], device)

        firsts = [
            (go(me, lows[q], 4 * q, right), go(me, highs[q], 4 * q + 1, left)) for q in range(pieces)
        ]
        yield
        rb = go(me, b, 4 * pieces, right)
        la = go(me, a, 4 * pieces + 1, left)
        yield
        onward = []
        for q, (ra, lb) in enumerate(firsts):
            ra.wait_recv()
            onward.append(go(fa, lows[q], 4 * q + 2, right))
            lb.wait_recv()
            onward.append(go(fb, highs[q], 4 * q + 3, left))
            yield
        rb.wait_recv()
        la.wait_recv()
        yield
        for copy in onward:
            copy.wait_recv()
        yield

    yring = ring4(ctg, y, 128, ys, yr, yr_dev, yl_dev)
    next(yring)
    next(yring)
    give_s = send(
        ovl.at[pl.ds((1 - l) * 8, 8)], sbuf.at[:, pl.ds(l * 8, 8)], hs.at[1], hr.at[1], twin
    )
    own_s.start()

    @pl.loop(0, 8)
    def _(i):
        mask_block((1 - l) * 8 + i)

    next(yring)
    hand = jnp.where(l == 0, 32, 8)
    takes = []
    for q in range(2):
        for copy in halo[q]:
            copy.wait_recv()
        given = cbuf.at[pl.ds(hand + 4 * q, 4)]
        takes.append(send(given, given, zs.at[3 * q + 2], zr.at[3 * q + 2], twin))
    own_h.wait()
    give_h.wait_recv()
    for copy in takes:
        copy.wait_recv()

    first = z * 16 - 16

    def picked(b, k):
        return cbuf[jnp.clip(neigh[b, k] - first, 0, 47)]

    def spmm(blocks, store, begin, end):
        @pl.loop(begin, end)
        def _(i):
            b = l * 8 + i
            total = jnp.zeros((128, 256), F32)
            for k in range(0, 16, 2):
                lhs = jnp.concatenate([blocks[i, k], blocks[i, k + 1]], axis=1)
                rhs = jnp.concatenate([picked(b, k), picked(b, k + 1)], axis=0)
                total += jnp.dot(lhs, rhs, preferred_element_type=F32)
            rows = lax.broadcasted_iota(jnp.int32, (128, 256), 0)
            store[pl.ds(pl.multiple_of(i * 128, 128), 128), :] = jnp.where(
                rows < sizes[b], total, 0.0
            ).astype(BF)

    slots = (x, lax.rem(x + 2, 4), lax.rem(x + 1, 4), lax.rem(x + 3, 4))
    swaps = {}

    def gram_part(p):
        rhs = hcg.at[slots[p]]

        @pl.loop(0, 2)
        def _(i):
            gsend[p, pl.ds(pl.multiple_of(i * 256, 256), 256), :] = jnp.dot(
                ctg[(1 - l) * 2 + i], rhs[...], preferred_element_type=F32
            )

        swaps[p] = send(gsend.at[p], grecv.at[p], ps.at[p], pr.at[p], twin)

        @pl.loop(0, 2)
        def _(i):
            gown[p, pl.ds(pl.multiple_of(i * 256, 256), 256), :] = jnp.dot(
                ctg[l * 2 + i], rhs[...], preferred_element_type=F32
            )

    def gram_add(p):
        swaps[p].wait_recv()
        gown[p] = gown[p] + grecv[p]

    def part(g, d):
        c = lax.rem(z + 8 + d, 8)
        return gown[g[0] : g[-1] + 1, pl.ds(pl.multiple_of(c * 64, 64), 64), :]

    def z_reduce(gi):
        g = GROUPS[gi]
        where = pl.ds(g[0], len(g))
        for p in g:
            gram_add(p)
        first = []
        for side, sign, one, two in ((0, 1, up, up2), (1, -1, down, down2)):
            rs_s[side, 0, where] = part(g, 3 * sign).astype(BF)
            rs_s4[side, where] = part(g, 4)[:, :, side * 128 : side * 128 + 128].astype(BF)
            n = 4 * side
            first.append((
                send(rs_s.at[side, 0, where], rs_r.at[side, 0, where], rss.at[gi, n], rsr.at[gi, n], one),
                send(rs_s4.at[side, where], rs_r4.at[side, where], rss.at[gi, n + 1], rsr.at[gi, n + 1], two),
            ))
        near = []
        for side, sign, one in ((0, 1, up), (1, -1, down)):
            rs_s[side, 1, where] = part(g, sign).astype(BF)
            n = 4 * side + 2
            near.append(send(
                rs_s.at[side, 1, where], rs_r.at[side, 1, where], rss.at[gi, n], rsr.at[gi, n], one
            ))
        yield
        for side, sign, two in ((0, 1, up2), (1, -1, down2)):
            three, four = first[side]
            lo, hi = side * 128, side * 128 + 128
            rest = slice(128, 256) if side == 0 else slice(0, 128)
            term = part(g, 2 * sign)
            three.wait_recv()
            four.wait_recv()
            term = term + rs_r[side, 0, where].astype(F32)
            rs_s[side, 2, where, :, lo:hi] = (
                term[:, :, lo:hi] + rs_r4[side, where].astype(F32)
            ).astype(BF)
            rs_s[side, 2, where, :, rest] = term[:, :, rest].astype(BF)
            n = 4 * side + 3
            near.append(send(
                rs_s.at[side, 2, where], rs_r.at[side, 2, where], rss.at[gi, n], rsr.at[gi, n], two
            ))
        yield
        whole = part(g, 0)
        for copy in near:
            copy.wait_recv()
        for side in range(2):
            whole = whole + rs_r[side, 1, where].astype(F32) + rs_r[side, 2, where].astype(F32)

        def rows(d):
            c = lax.rem(z + 8 + d, 8)
            return pl.ds(pl.multiple_of(l * 512 + c * 64, 64), 64)

        gram[where, rows(0), :] = (whole * (1.0 / 16384.0)).astype(BF)
        twins = []

        def to_twin(d, n):
            ref = gram.at[where, rows(d), :]
            twins.append(send(ref, ref, agps.at[gi, n], agpr.at[gi, n], twin))

        def hop(d, n, device, cols=slice(None)):
            ref = gram.at[where, rows(d), cols]
            return send(ref, ref, ags.at[gi, n], agr.at[gi, n], device)

        far = [hop(0, 0, up2), hop(0, 1, down2)]
        close = [hop(0, 2, up), hop(0, 3, down)]
        to_twin(0, 0)
        yield
        last = []
        for side, sign, one, two in ((0, -1, up, up2), (1, 1, down, down2)):
            far[side].wait_recv()
            last.append(hop(2 * sign, 4 + side, one))
            last.append(hop(2 * sign, 6 + side, two, pl.ds(side * 128, 128)))
        for side, sign in ((0, -1), (1, 1)):
            to_twin(2 * sign, 1 + side)
            close[side].wait_recv()
            to_twin(sign, 3 + side)
        yield
        for n, copy in enumerate(last):
            copy.wait_recv()
            if n % 2 == 0:
                to_twin(3 if n else -3, 5 + n // 2)
        to_twin(4, 7)
        yield
        for copy in twins:
            copy.wait_recv()
        yield

    spmm(hbuf, hcg.at[x], 0, 8)
    xring = ring4(hcg, x, 512, xs, xr, xr_dev, xl_dev, 2)
    next(xring)
    next(xring)
    next(yring)
    next(yring)
    own_s.wait()
    give_s.wait_recv()
    gram_part(0)
    spmm(sbuf, scg.at[y], 0, 8)
    sring = ring4(scg, y, 512, ss, sr, yr_dev, yl_dev)
    next(sring)
    next(sring)
    reducers = [z_reduce(gi) for gi in range(4)]

    def step(*which):
        for gi in which:
            next(reducers[gi])

    step(0)
    next(xring)
    step(0)
    next(xring)
    next(xring)
    gram_part(2)
    gram_part(3)
    step(0)
    step(2, 3)
    next(sring)
    step(0)
    step(2, 3)
    next(xring)
    gram_part(1)
    step(2, 3)
    step(1)
    step(0)
    step(2, 3)
    step(1)
    step(0)
    step(2, 3)
    step(1)
    next(sring)
    next(sring)
    step(2, 3)

    def project(p, i):
        total = jnp.zeros((512, 256), F32)
        for k in range(4):
            total += jnp.dot(
                scg[k, pl.ds(i * 512, 512), :], gram[p, k * 256 : (k + 1) * 256, :],
                preferred_element_type=F32,
            )
        return total

    nb_s[0, 1] = project(2, 1).astype(BF)
    near = [send(nb_s.at[0, 1], nb_r.at[0, 1], fs.at[4], fr.at[4], xr_dev)]
    nb_s[1, 0] = project(3, 0).astype(BF)
    near.append(send(nb_s.at[1, 0], nb_r.at[1, 0], fs.at[5], fr.at[5], xl_dev))
    step(1)
    racc[0] = project(2, 0)
    racc[1] = project(3, 1)
    step(1)
    step(1)
    pieces = (pl.ds(0, 256), pl.ds(256, 256))
    far = []
    for side, device in ((0, xr_dev), (1, xl_dev)):
        opp_s[side] = project(1, side).astype(BF)
        for q, rows in enumerate(pieces):
            n = 2 * q + side
            far.append(send(opp_s.at[side, rows], opp_r.at[side, rows], fs.at[n], fr.at[n], device))
    for i in range(2):
        own[i] = hcg[x, pl.ds(i * 512, 512), :].astype(F32) - project(0, i)
    for q, rows in enumerate(pieces):
        for side, device in ((0, xr_dev), (1, xl_dev)):
            far[2 * side + q].wait_recv()
            nb_s[side, side, rows] = (racc[side, rows] + opp_r[side, rows].astype(F32)).astype(BF)
            n = 6 + 2 * q + side
            near.append(send(
                nb_s.at[side, side, rows], nb_r.at[side, side, rows], fs.at[n], fr.at[n], device
            ))
    for copy in near:
        copy.wait_recv()
    for i in range(2):
        out[pl.ds(i * 512, 512), :] = own[i] - nb_r[0, i].astype(F32) - nb_r[1, i].astype(F32)
    for copy in sent:
        copy.wait_send()


def body(coeffs, block_sizes, neighbours, ham_blocks, ovl_blocks):
    vmem = pltpu.VMEM
    dma = pltpu.SemaphoreType.DMA
    n = len(GROUPS)
    smem = pl.BlockSpec(memory_space=pltpu.SMEM)
    hbm = pl.BlockSpec(memory_space=pl.ANY)
    return pl.pallas_call(
        kernel,
        out_shape=jax.ShapeDtypeStruct((1024, 256), F32),
        in_specs=[smem, smem, hbm, hbm, hbm],
        out_specs=pl.BlockSpec(memory_space=pltpu.VMEM),
        scratch_shapes=[
            vmem((2048, 256), BF),
            vmem((48, 128, 256), BF),
            vmem((8, 16, 128, 128), BF),
            vmem((8, 16, 128, 128), BF),
            vmem((4, 256, 1024), BF),
            vmem((4, 1024, 256), BF),
            vmem((4, 1024, 256), BF),
            vmem((4, 512, 256), F32),
            vmem((4, 512, 256), F32),
            vmem((4, 512, 256), F32),
            vmem((4, 1024, 256), BF),
            vmem((2, 3, 4, 64, 256), BF),
            vmem((2, 3, 4, 64, 256), BF),
            vmem((2, 4, 64, 128), BF),
            vmem((2, 4, 64, 128), BF),
            vmem((2, 512, 256), BF),
            vmem((2, 512, 256), BF),
            vmem((2, 2, 512, 256), BF),
            vmem((2, 2, 512, 256), BF),
            vmem((2, 512, 256), F32),
            vmem((2, 512, 256), F32),
            dma((3,)),
            dma((6,)), dma((6,)),
            dma((2,)), dma((2,)),
            dma((6,)), dma((6,)),
            dma((10,)), dma((10,)),
            dma((6,)), dma((6,)),
            dma((4,)), dma((4,)),
            dma((n, 8)), dma((n, 8)),
            dma((n, 8)), dma((n, 8)),
            dma((n, 8)), dma((n, 8)),
            dma((10,)), dma((10,)),
        ],
        compiler_params=pltpu.CompilerParams(
            collective_id=0, has_side_effects=True, vmem_limit_bytes=56 * 2**20
        ),
        cost_estimate=pl.CostEstimate(
            flops=6 * 2**30, bytes_accessed=12 * 2**20, transcendentals=0
        ),
        name="block_sparse_residual",
    )(block_sizes, neighbours, coeffs, ham_blocks, ovl_blocks)


def solution(mesh):
    return jax.shard_map(
        body,
        mesh=mesh,
        in_specs=(
            P("row", "col"),
            P("row"),
            P("row", None),
            P("row", "layer", None, None),
            P("row", "layer", None, None),
        ),
        out_specs=P(("row", "layer"), "col"),
        check_vma=False,
    )
```
